32 devices in a mesh: dp: 8 (over z, x), tensor: 4 (over y, core).
Axes of the slice: x: 2, y: 2, z: 4, core: 2. Of those that a mesh axis runs over, the one named last changes fastest.
Arguments:
- layer_input: bfloat16 [16384, 768], P(('dp', 'tensor')), may hold values from -6 to 6
- out_cotangent: bfloat16 [16384, 768], P(('dp', 'tensor')), may hold values from -6 to 6
- qkv_weight: bfloat16 [3, 768, 768], P(None, None, 'tensor'), may hold values from -0.21875 to 0.21875
- qv_bias: bfloat16 [2, 768], P(None, 'tensor'), may hold values from -1 to 1
- out_weight: bfloat16 [768, 768], P('tensor'), may hold values from -0.875 to 0.875
- out_bias: bfloat16 [768], replicated, may hold values from -1 to 1
- norm1_gain: bfloat16 [768], replicated, may hold values from 0.5 to 1.5
- norm1_bias: bfloat16 [768], replicated, may hold values from -1 to 1
- up_weight: bfloat16 [768, 3072], P(None, 'tensor'), may hold values from -0.21875 to 0.21875
- up_bias: bfloat16 [3072], P('tensor'), may hold values from -1 to 1
- down_weight: bfloat16 [3072, 768], P('tensor'), may hold values from -0.15625 to 0.15625
- down_bias: bfloat16 [768], replicated, may hold values from -1 to 1
- norm2_gain: bfloat16 [768], replicated, may hold values from 0.5 to 1.5
- norm2_bias: bfloat16 [768], replicated, may hold values from -1 to 1
- cluster_perm: int32 [32, 12, 512], P('dp', 'tensor'), may hold values from 0 to 511, each once within a row
- segment_ids: int32 [32, 512], P('dp'), may hold values from 0 to 3, never falling along the last dimension, each value on 1 to 256 neighbouring positions
Outputs:
- layer_output: bfloat16 [16384, 768], P(('dp', 'tensor'))
- input_grad: bfloat16 [16384, 768], P(('dp', 'tensor'))
- qkv_weight_grad: float32 [3, 768, 768], P(None, None, 'tensor')
- qv_bias_grad: float32 [2, 768], P(None, 'tensor')
- out_weight_grad: float32 [768, 768], P('tensor')
- out_bias_grad: float32 [768], replicated
- norm1_gain_grad: float32 [768], replicated
- norm1_bias_grad: float32 [768], replicated
- up_weight_grad: float32 [768, 3072], P(None, 'tensor')
- up_bias_grad: float32 [3072], P('tensor')
- down_weight_grad: float32 [3072, 768], P('tensor')
- down_bias_grad: float32 [768], replicated
- norm2_gain_grad: float32 [768], replicated
- norm2_bias_grad: float32 [768], replicated
The draws below stay inside these ranges and needn't reach their ends.
Inputs may be any that keep to these rules, and one draw needn't show every extreme that they name: `cluster_perm`: each row of a head lists every position of its packed row once. `segment_ids`: never falls along a packed row; each id covers 1 to 256 consecutive positions.
All inputs are finite; a program needn't handle non-finite values.
Results may differ from the reference program's by a relative error of at most 0.02.
Values may be sent and summed in bfloat16 or wider, within the bound.
No kernel may reach another device: no remote copies, remote signals or barrier semaphores. Data moves between devices by JAX's collectives and lax.ppermute only.
A program may use at most 128 MiB of HBM per device.

```python
import math
import jax
import jax.numpy as jnp
import numpy as np
from jax import lax

D = 768
HEADS = 12
HEAD_DIM = 64
FF = 3072
LEN = 512
CLUSTER = 128
ALL_SEQS = 32
TOKENS = 16384


def levels(key, extent, split, smallest, top_value):
    def one(axis_at, shards_of):
        heights = jax.random.uniform(jax.random.fold_in(jax.random.fold_in(key, 6), axis_at), (shards_of,), jnp.float32, smallest / len(split), top_value / len(split))
        return jnp.repeat(jnp.exp(heights), extent[axis_at] // shards_of).reshape((-1,) + (1,) * (len(extent) - axis_at - 1))

    level = one(*split[0])
    for cut in split[1:]:
        level = level * one(*cut)
    return level


def split_up(number_of, total, limit, skew):
    portions = [(1 << 20) // math.isqrt(grade ** skew) + 1 for grade in range(2, number_of + 1)]
    spare, holding = total - limit - (number_of - 1), [1] * (number_of - 1)
    while spare > 0:
        movable = [i for i in range(number_of - 1) if holding[i] < limit]
        whole, budget = sum([portions[i] for i in movable]), spare
        for i in movable:
            more = min(limit - holding[i], max(1, budget * portions[i] // whole), spare)
            holding[i] = holding[i] + more
            spare = spare - more
    return np.array([limit] + holding)


def uneven_parts(key, count, total, bound, slope):
    if count == 2:
        one = jax.random.randint(key, (), max(1, total - bound), min(bound, total - 1) + 1)
        return jnp.stack([one, total - one])
    sizes = jnp.asarray(split_up(count, total, bound, slope), jnp.int32)
    twos = (count - 1) // 2
    giver, receiver = sizes[1:1 + 2 * twos:2], sizes[2:2 + 2 * twos:2]
    margin = jnp.minimum(giver - 1, bound - receiver)
    moved = jax.random.randint(jax.random.fold_in(key, 1), (twos,), 0, 1 << 20) % (margin + 1)
    sizes = sizes.at[1:1 + 2 * twos:2].set(giver - moved).at[2:2 + 2 * twos:2].set(receiver + moved)
    return sizes[jax.random.permutation(jax.random.fold_in(key, 2), count)]


def normal_values(stream_key, extent, spread, most, pieces=(), kind=jnp.bfloat16):
    entries = jax.random.normal(stream_key, extent, jnp.float32) * spread
    if len(pieces) > 0:
        entries = levels(stream_key, extent, pieces, -0.22, 0.18) * entries
    return jnp.clip(entries, min=-most, max=most).astype(kind)


def setup_inputs(seed: int = 0) -> dict:
    key_of = jax.random.split(jax.random.key(seed), 17)
    return {
        "layer_input": normal_values(key_of[0], (TOKENS, D), 1.0, 6.0, ((0, 32),)),
        "out_cotangent": normal_values(key_of[1], (TOKENS, D), 1.0, 6.0, ((0, 32),)),
        "qkv_weight": normal_values(key_of[2], (3, D, D), D ** -0.5, 0.21875, ((2, 4),)),
        "qv_bias": normal_values(key_of[3], (2, D), 0.2, 1.0, ((1, 4),)),
        "out_weight": normal_values(key_of[4], (D, D), (D // 16) ** -0.5, 0.875, ((0, 4),)),
        "out_bias": normal_values(key_of[5], (D,), 0.2, 1.0),
        "norm1_gain": jnp.clip(1.0 + 0.1 * jax.random.normal(key_of[6], (D,), jnp.float32), 0.5, 1.5).astype(jnp.bfloat16),
        "norm1_bias": normal_values(key_of[7], (D,), 0.2, 1.0),
        "up_weight": normal_values(key_of[8], (D, FF), D ** -0.5, 0.21875, ((1, 4),)),
        "up_bias": normal_values(key_of[9], (FF,), 0.2, 1.0, ((0, 4),)),
        "down_weight": normal_values(key_of[10], (FF, D), (FF // 2) ** -0.5, 0.15625, ((0, 4),)),
        "down_bias": normal_values(key_of[11], (D,), 0.2, 1.0),
        "norm2_gain": jnp.clip(1.0 + 0.1 * jax.random.normal(key_of[12], (D,), jnp.float32), 0.5, 1.5).astype(jnp.bfloat16),
        "norm2_bias": normal_values(key_of[13], (D,), 0.2, 1.0),
        "cluster_perm": jax.vmap(lambda own: jax.random.permutation(own, LEN))(jax.random.split(key_of[14], ALL_SEQS * HEADS)).reshape((ALL_SEQS, HEADS, LEN)).astype(jnp.int32),
        "segment_ids": jax.vmap(lambda own: jnp.searchsorted(jnp.cumsum(uneven_parts(own, 4, LEN, LEN // 2, 0)), jnp.arange(LEN), side="right"))(jax.random.split(key_of[15], ALL_SEQS)).reshape((ALL_SEQS, LEN)).astype(jnp.int32),
    }


@jax.custom_vjp
def low(v):
    return lax.optimization_barrier(v.astype(jnp.bfloat16)).astype(jnp.float32)

@jax.custom_vjp
def low_back(v):
    return v

def low_keep(v):
    return (low(v), None)

def low_pass(kept, grad):
    return (grad,)

def back_keep(v):
    return (v, None)

def back_low(kept, grad):
    return (low(grad),)
low.defvjp(low_keep, low_pass)
low_back.defvjp(back_keep, back_low)
highest = lax.Precision.HIGHEST
norm_eps = 1e-12
inv_root_two = 0.7071067811865476

def rounded(v):
    return low(low_back(v))

def layer_norm(values, gain, shift):
    center = values - lax.optimization_barrier(jnp.mean(values, axis=-1, keepdims=True))
    variance = lax.optimization_barrier(jnp.mean(center * center, axis=-1, keepdims=True))
    return center * lax.rsqrt(variance + norm_eps) * gain + shift

def gelu_value(v):
    return 0.5 * v * (1.0 + lax.erf(v * inv_root_two))

def attend_sequence(member):
    query_rows, key_rows, value_rows, order, seg_row = member
    score_scale = 1.0 / math.sqrt(HEAD_DIM)

    def arrange(field):
        shaped = field.reshape(LEN, HEADS, HEAD_DIM).transpose(1, 0, 2)
        permuted = jnp.take_along_axis(shaped, order[:, :, None], axis=1)
        return permuted.reshape(HEADS, LEN // CLUSTER, CLUSTER, HEAD_DIM)
    queries = arrange(query_rows)
    key_blocks = arrange(key_rows)
    value_blocks = arrange(value_rows)
    seg_blocks = jnp.take(seg_row, order).reshape(HEADS, LEN // CLUSTER, CLUSTER)
    visible = seg_blocks[..., :, None] == seg_blocks[..., None, :]
    raw_scores = low_back(jnp.einsum('hcid,hcjd->hcij', queries, key_blocks, precision=highest) * score_scale)
    masked = jnp.where(visible, raw_scores, -1000000000.0)
    row_max = lax.optimization_barrier(jnp.max(masked, axis=-1, keepdims=True))
    exp_scores = jnp.exp(masked - row_max)
    probs = low(exp_scores / lax.optimization_barrier(jnp.sum(exp_scores, axis=-1, keepdims=True)))
    blocks = jnp.einsum('hcij,hcjd->hcid', probs, value_blocks, precision=highest)
    flattened = blocks.reshape(HEADS, LEN, HEAD_DIM)
    inverse_order = jnp.argsort(order, axis=-1).astype(jnp.int32)
    restored = jnp.take_along_axis(flattened, inverse_order[:, :, None], axis=1)
    return restored.transpose(1, 0, 2).reshape(LEN, D)

def forward(tokens, params, order, seg_rows):
    qkv_weight, qv_bias, out_weight, out_bias, norm1_gain, norm1_bias, up_weight, up_bias, down_weight, down_bias, norm2_gain, norm2_bias = params
    group_seqs = order.shape[0]
    queries = rounded(jnp.dot(tokens, qkv_weight[0], precision=highest) + qv_bias[0])
    key_rows = rounded(jnp.dot(tokens, qkv_weight[1], precision=highest))
    value_rows = rounded(jnp.dot(tokens, qkv_weight[2], precision=highest) + qv_bias[1])
    shape_three = (group_seqs, LEN, D)
    context = lax.map(jax.checkpoint(attend_sequence), (queries.reshape(shape_three), key_rows.reshape(shape_three), value_rows.reshape(shape_three), order, seg_rows))
    context = rounded(context.reshape(group_seqs * LEN, D))
    attn_sum = low_back(jnp.dot(context, out_weight, precision=highest))
    resid_a = tokens + attn_sum + out_bias
    middle = layer_norm(resid_a, norm1_gain, norm1_bias)
    hidden_pre = low_back(jnp.dot(low(middle), up_weight, precision=highest) + up_bias)
    hidden = low(gelu_value(hidden_pre))
    ffn_sum = low_back(jnp.dot(hidden, down_weight, precision=highest))
    return layer_norm(middle + ffn_sum + down_bias, norm2_gain, norm2_bias)

def reference(layer_input, out_cotangent, qkv_weight, qv_bias, out_weight, out_bias, norm1_gain, norm1_bias, up_weight, up_bias, down_weight, down_bias, norm2_gain, norm2_bias, cluster_perm, segment_ids):
    weights = tuple((member.astype(jnp.float32) for member in (qkv_weight, qv_bias, out_weight, out_bias, norm1_gain, norm1_bias, up_weight, up_bias, down_weight, down_bias, norm2_gain, norm2_bias)))
    seq_total = cluster_perm.shape[0]
    group_seqs = math.gcd(seq_total, 8)
    step_count = seq_total // group_seqs
    inputs = layer_input.reshape(step_count, group_seqs * LEN, D)
    cotangents = out_cotangent.reshape(step_count, group_seqs * LEN, D)
    orders = cluster_perm.reshape(step_count, group_seqs, HEADS, LEN)
    segments = segment_ids.reshape(step_count, group_seqs, LEN)

    def scan_step(totals_in, member):
        rows_in, cotangent, order, seg_rows = member

        def forward_run(tokens, *params):
            return forward(tokens, params, order, seg_rows)
        result, pullback = jax.vjp(forward_run, rows_in.astype(jnp.float32), *weights)
        gradients = pullback(cotangent.astype(jnp.float32))
        totals_out = tuple((running + partial_value for running, partial_value in zip(totals_in, gradients[1:])))
        return (totals_out, (result.astype(jnp.bfloat16), gradients[0].astype(jnp.bfloat16)))
    initial = tuple((jnp.zeros(member.shape, jnp.float32) for member in weights))
    totals_out, (outputs, input_grads) = lax.scan(scan_step, initial, (inputs, cotangents, orders, segments))
    qkv_grad, qv_grad, out_w_grad, out_b_grad, gain1_grad, bias1_grad, up_w_grad, up_b_grad, down_w_grad, down_b_grad, gain2_grad, bias2_grad = totals_out
    return (outputs.reshape(seq_total * LEN, D), input_grads.reshape(seq_total * LEN, D), qkv_grad, qv_grad, out_w_grad, out_b_grad, gain1_grad, bias1_grad, up_w_grad, up_b_grad, down_w_grad, down_b_grad, gain2_grad, bias2_grad)
```

```python
import math

import jax
import jax.numpy as jnp
from jax import lax
from jax.experimental import pallas as pl
from jax.experimental.pallas import tpu as pltpu
from jax.sharding import PartitionSpec as P

HEAD_DIM = 64
CLUSTER = 128
NORM_EPS = 1e-12
MASKED = -1000000000.0
ROOT_HALF = 0.7071067811865476
INV_ROOT_TWO_PI = 0.3989422804014327
SCALE = 1.0 / math.sqrt(HEAD_DIM)
SLOT = 4 * HEAD_DIM
EXTRA = 64
F32 = jnp.float32
BF16 = jnp.bfloat16


def mm(a, b):
    return jnp.dot(a, b, preferred_element_type=F32)


def mm_nt(a, b):
    return lax.dot_general(a, b, (((1,), (1,)), ((), ())), preferred_element_type=F32)


def mm_tn(a, b):
    return lax.dot_general(a, b, (((0,), (0,)), ((), ())), preferred_element_type=F32)


def call(body, outs, scratch, flops, *args):
    shapes = [jax.ShapeDtypeStruct(s, t) for s, t in outs]
    moved = sum(math.prod(s) * jnp.dtype(t).itemsize for s, t in outs)
    moved += sum(a.size * a.dtype.itemsize for a in args)
    spec = {True: pl.BlockSpec(memory_space=pltpu.SMEM), False: pl.BlockSpec(memory_space=pltpu.VMEM)}
    return pl.pallas_call(
        body,
        out_shape=shapes,
        in_specs=[spec[a.dtype == jnp.int32] for a in args],
        out_specs=[pl.BlockSpec(memory_space=pltpu.VMEM)] * len(outs),
        scratch_shapes=scratch,
        cost_estimate=pl.CostEstimate(flops=int(flops), bytes_accessed=int(moved), transcendentals=0),
        compiler_params=pltpu.CompilerParams(vmem_limit_bytes=48 * 1024 * 1024),
    )(*args)


def norm(values):
    center = values - jnp.mean(values, axis=-1, keepdims=True)
    inverse = lax.rsqrt(jnp.mean(center * center, axis=-1, keepdims=True) + NORM_EPS)
    return center * inverse, inverse


def norm_back(grad_in, normed, inverse, gain):
    scaled = grad_in * gain
    return inverse * (
        scaled
        - jnp.mean(scaled, axis=-1, keepdims=True)
        - normed * jnp.mean(scaled * normed, axis=-1, keepdims=True)
    )


def colsum(v):
    return jnp.sum(v, axis=0, keepdims=True)


def assemble(scratch, half_ref, relayed_ref, side):
    rows = half_ref.shape[0]
    here, there = half_ref[...], relayed_ref[...]
    scratch[0:rows, :] = jnp.where(side == 0, here, there)
    scratch[rows : 2 * rows, :] = jnp.where(side == 0, there, here)


def pack_kernel(qkv_ref, out_ref, packed_ref):
    turned = out_ref[...].astype(F32).T.astype(BF16)
    heads = qkv_ref.shape[2] // HEAD_DIM
    for h in range(heads):
        cut = slice(h * HEAD_DIM, (h + 1) * HEAD_DIM)
        packed_ref[:, h * SLOT : (h + 1) * SLOT] = jnp.concatenate(
            [qkv_ref[0, :, cut], qkv_ref[1, :, cut], qkv_ref[2, :, cut], turned[:, cut]], axis=1
        )


def unpack_kernel(packed_ref, qkv_ref, out_ref, vec_ref):
    width = packed_ref.shape[1]
    heads = width // SLOT
    rows = qkv_ref.shape[1]
    for member in range(3):
        qkv_ref[member] = jnp.concatenate(
            [
                packed_ref[0:rows, h * SLOT + member * HEAD_DIM : h * SLOT + (member + 1) * HEAD_DIM]
                for h in range(heads)
            ],
            axis=1,
        ).astype(F32)
    out_ref[...] = (
        jnp.concatenate(
            [packed_ref[0:rows, h * SLOT + 3 * HEAD_DIM : (h + 1) * SLOT] for h in range(heads)], axis=1
        )
        .astype(F32)
        .T
    )
    vec_ref[...] = packed_ref[rows : rows + 16, :].astype(F32)


def order_table(order_ref, turned_ref, h):
    length = order_ref.shape[1]
    lane = lax.broadcasted_iota(jnp.int32, (length, length), 1).astype(F32)
    sub = lax.broadcasted_iota(jnp.int32, (length, length), 0).astype(F32)
    by_place = jnp.where(turned_ref[:, h : h + 1] == lane, 1.0, 0.0).astype(BF16)
    by_position = jnp.where(order_ref[h : h + 1, :] == sub, 1.0, 0.0).astype(BF16)
    return by_place, by_position


def attend(tokens, weight_ref, bias_ref, order_ref, turned_ref, group, fields_ref, probs_ref):
    heads = weight_ref.shape[1] // SLOT
    length = tokens.shape[0]
    seg_at = order_ref.shape[0] - 2
    lanes = lax.broadcasted_iota(jnp.int32, (length, SLOT), 1)
    out = []
    for h in range(heads):
        at = group * heads + h
        by_place, by_position = order_table(order_ref, turned_ref, at)
        fields = mm(tokens, weight_ref[:, h * SLOT : (h + 1) * SLOT]) + bias_ref[at : at + 1, :]
        fields = jnp.where(lanes < 3 * HEAD_DIM, fields, turned_ref[:, seg_at : seg_at + 1]).astype(BF16)
        placed_wide = mm(by_place, fields)
        placed = placed_wide.astype(BF16)
        fields_ref[at] = placed
        seg_col = placed_wide[:, SLOT - 1 : SLOT]
        seg_row = mm(order_ref[...].astype(BF16), by_position)[seg_at : seg_at + 1, :]
        blocks = []
        for c in range(length // CLUSTER):
            cut = slice(c * CLUSTER, (c + 1) * CLUSTER)
            queries = placed[cut, 0:HEAD_DIM]
            keys = placed[cut, HEAD_DIM : 2 * HEAD_DIM]
            values = placed[cut, 2 * HEAD_DIM : 3 * HEAD_DIM]
            scores = mm_nt(queries, keys) * SCALE
            scores = jnp.where(seg_col[cut, :] == seg_row[:, cut], scores, MASKED)
            raised = jnp.exp(scores - jnp.max(scores, axis=-1, keepdims=True))
            probs = (raised / jnp.sum(raised, axis=-1, keepdims=True)).astype(BF16)
            probs_ref[at, cut, :] = probs
            blocks.append(mm(probs, values).astype(BF16))
        out.append(mm(by_position, jnp.concatenate(blocks, axis=0)).astype(BF16))
    return jnp.concatenate(out, axis=1)


def turned_out(weight_ref):
    heads = weight_ref.shape[1] // SLOT
    return jnp.concatenate([weight_ref[:, h * SLOT + 3 * HEAD_DIM : (h + 1) * SLOT] for h in range(heads)], axis=1)


def near_attention(
    x_ref, w0_ref, w1_ref, bias_ref, order_ref, turned_ref, fields_ref, probs_ref, ctx_ref, sum_ref
):
    tokens = x_ref[...]
    total = None
    for group, w_ref in enumerate((w0_ref, w1_ref)):
        ctx = attend(tokens, w_ref, bias_ref, order_ref, turned_ref, group, fields_ref, probs_ref)
        ctx_ref[group] = ctx
        part = mm_nt(ctx, turned_out(w_ref))
        total = part if total is None else total + part
    sum_ref[...] = total


def far_attention(
    side_ref, x_ref, a2_ref, b2_ref, a3_ref, b3_ref, bias_ref, order_ref, turned_ref, sum_ref, vec_ref,
    fields_ref, probs_ref, ctx_ref, low_ref, normed_ref, inverse_ref, w_ref,
):
    tokens = x_ref[...]
    side = side_ref[0]
    total = sum_ref[...]
    for group, (a_ref, b_ref) in enumerate(((a2_ref, b2_ref), (a3_ref, b3_ref))):
        assemble(w_ref.at[group], a_ref, b_ref, side)
        ctx = attend(tokens, w_ref.at[group], bias_ref, order_ref, turned_ref, group, fields_ref, probs_ref)
        ctx_ref[group] = ctx
        total = total + mm_nt(ctx, turned_out(w_ref.at[group]))
    normed, inverse = norm(tokens.astype(F32) + total + vec_ref[0:1, :])
    low_ref[...] = (normed * vec_ref[1:2, :] + vec_ref[2:3, :]).astype(BF16)
    normed_ref[...] = normed
    inverse_ref[...] = inverse


def hidden_units(low_ref, up_ref, shift, hidden_ref, slope_ref):
    length = low_ref.shape[0]
    step = 128
    for r in range(0, length, step):
        v = mm(low_ref[r : r + step, :], up_ref[...]) + shift
        half = 0.5 + 0.5 * lax.erf(v * ROOT_HALF)
        hidden_ref[r : r + step, :] = (v * half).astype(BF16)
        slope_ref[r : r + step, :] = (half + v * jnp.exp(-0.5 * v * v) * INV_ROOT_TWO_PI).astype(BF16)


def near_forward(low_ref, u0_ref, u1_ref, d0_ref, d1_ref, shift_ref, hidden_ref, slope_ref, sum_ref):
    hidden_units(low_ref, u0_ref, shift_ref[0:1, :], hidden_ref.at[0], slope_ref.at[0])
    hidden_units(low_ref, u1_ref, shift_ref[1:2, :], hidden_ref.at[1], slope_ref.at[1])
    sum_ref[...] = mm(hidden_ref[0], d0_ref[...]) + mm(hidden_ref[1], d1_ref[...])


def far_up(side_ref, low_ref, a2_ref, b2_ref, a3_ref, b3_ref, shift_ref, hidden_ref, slope_ref, u_ref):
    for group, (a_ref, b_ref) in enumerate(((a2_ref, b2_ref), (a3_ref, b3_ref))):
        assemble(u_ref, a_ref, b_ref, side_ref[0])
        hidden_units(low_ref, u_ref, shift_ref[group : group + 1, :], hidden_ref.at[group], slope_ref.at[group])


def far_down(
    side_ref, hidden_ref, a2_ref, b2_ref, a3_ref, b3_ref, sum_ref, normed_a_ref, cot_ref, vec_ref,
    out_ref, grad_ref, grad_low_ref, sums_ref, d_ref,
):
    total = sum_ref[...]
    for group, (a_ref, b_ref) in enumerate(((a2_ref, b2_ref), (a3_ref, b3_ref))):
        assemble(d_ref, a_ref, b_ref, side_ref[0])
        total = total + mm(hidden_ref[group], d_ref[...])
    middle = normed_a_ref[...] * vec_ref[1:2, :] + vec_ref[2:3, :]
    normed, inverse = norm(middle + total + vec_ref[3:4, :])
    out_ref[...] = (normed * vec_ref[4:5, :] + vec_ref[5:6, :]).astype(BF16)
    cot = cot_ref[...].astype(F32)
    grad = norm_back(cot, normed, inverse, vec_ref[4:5, :])
    grad_ref[...] = grad
    grad_low_ref[...] = grad.astype(BF16)
    sums_ref[...] = jnp.zeros_like(sums_ref)
    sums_ref[0:1, :] = colsum(cot * normed)
    sums_ref[1:2, :] = colsum(cot)
    sums_ref[2:3, :] = colsum(grad)


def down_grads(hidden_ref, grad_low_ref, first_ref, second_ref):
    first_ref[...] = mm_tn(hidden_ref[1], grad_low_ref[...]).astype(BF16)
    second_ref[...] = mm_tn(hidden_ref[0], grad_low_ref[...]).astype(BF16)


def up_grads(grad_low_ref, low_ref, slope, down_ref, up_ref, out_ref):
    pre = (mm_nt(grad_low_ref[...], down_ref[...]) * slope).astype(BF16)
    out_ref[...] = mm_tn(low_ref[...], pre).astype(BF16)
    return mm_nt(pre, up_ref[...]), colsum(pre.astype(F32))


def far_up_grads(
    side_ref, grad_low_ref, low_ref, slope_ref, d2a_ref, d2b_ref, d3a_ref, d3b_ref, u2a_ref, u2b_ref, u3a_ref, u3b_ref,
    g3_ref, g2_ref, mid_ref, shift_ref, d_ref, u_ref,
):
    side = side_ref[0]
    total = None
    shift_ref[...] = jnp.zeros_like(shift_ref)
    for group, halves, out_ref in (
        (1, (d3a_ref, d3b_ref, u3a_ref, u3b_ref), g3_ref),
        (0, (d2a_ref, d2b_ref, u2a_ref, u2b_ref), g2_ref),
    ):
        assemble(d_ref, halves[0], halves[1], side)
        assemble(u_ref, halves[2], halves[3], side)
        part, sums = up_grads(grad_low_ref, low_ref, slope_ref[group].astype(F32), d_ref, u_ref, out_ref)
        shift_ref[group : group + 1, :] = sums
        total = part if total is None else total + part
    mid_ref[...] = total


def near_up_grads(
    grad_low_ref, low_ref, slope_ref, d0_ref, d1_ref, u0_ref, u1_ref, mid_ref, grad_b_ref, normed_ref, inverse_ref,
    vec_ref, g1_ref, g0_ref, grad_ref, grad_out_ref, shift_ref, sums_ref,
):
    total = mid_ref[...] + grad_b_ref[...]
    shift_ref[...] = jnp.zeros_like(shift_ref)
    for group, d_ref, u_ref, out_ref in ((1, d1_ref, u1_ref, g1_ref), (0, d0_ref, u0_ref, g0_ref)):
        part, sums = up_grads(grad_low_ref, low_ref, slope_ref[group].astype(F32), d_ref, u_ref, out_ref)
        shift_ref[group : group + 1, :] = sums
        total = total + part
    normed = normed_ref[...]
    grad = norm_back(total, normed, inverse_ref[...], vec_ref[1:2, :])
    grad_ref[...] = grad
    grad_out_ref[...] = grad.astype(BF16)
    sums_ref[...] = jnp.zeros_like(sums_ref)
    sums_ref[0:1, :] = colsum(total * normed)
    sums_ref[1:2, :] = colsum(total)
    sums_ref[2:3, :] = colsum(grad)


def attend_back(tokens, grad_out, weight_ref, order_ref, turned_ref, group, fields_ref, probs_ref, ctx_ref, out_ref, tok_ref):
    heads = weight_ref.shape[1] // SLOT
    length, width = tokens.shape
    grad_ctx = mm(grad_out, turned_out(weight_ref)).astype(BF16)
    out_grad = mm_tn(grad_out, ctx_ref[group])
    for h in range(heads):
        at = group * heads + h
        by_place, by_position = order_table(order_ref, turned_ref, at)
        grads = mm(by_place, grad_ctx[:, h * HEAD_DIM : (h + 1) * HEAD_DIM]).astype(BF16)
        placed = fields_ref[at]
        rows = []
        for c in range(length // CLUSTER):
            cut = slice(c * CLUSTER, (c + 1) * CLUSTER)
            queries = placed[cut, 0:HEAD_DIM]
            keys = placed[cut, HEAD_DIM : 2 * HEAD_DIM]
            values = placed[cut, 2 * HEAD_DIM : 3 * HEAD_DIM]
            low = probs_ref[at, cut, :]
            probs = low.astype(F32)
            grad_probs = mm_nt(grads[cut, :], values)
            delta = jnp.sum(grad_probs * probs, axis=-1, keepdims=True)
            grad_scores = (probs * (grad_probs - delta)).astype(BF16)
            rows.append(
                jnp.concatenate(
                    [
                        mm(grad_scores, keys) * SCALE,
                        mm_tn(grad_scores, queries) * SCALE,
                        mm_tn(low, grads[cut, :]),
                        jnp.zeros((CLUSTER, HEAD_DIM), F32),
                    ],
                    axis=1,
                ).astype(BF16)
            )
        tok_ref[:, h * SLOT : (h + 1) * SLOT] = mm(by_position, jnp.concatenate(rows, axis=0)).astype(BF16)
    grad = mm_tn(tokens, tok_ref[...])
    for h in range(heads):
        out_ref[0:width, h * SLOT : (h + 1) * SLOT] = jnp.concatenate(
            [grad[:, h * SLOT : h * SLOT + 3 * HEAD_DIM], out_grad[:, h * HEAD_DIM : (h + 1) * HEAD_DIM]], axis=1
        ).astype(BF16)
    return mm_nt(tok_ref[...], weight_ref[...]), colsum(tok_ref[...].astype(F32))


def put_vectors(out_ref, rows, sums_b, sums_a, shift, fields):
    zero = jnp.zeros((EXTRA - 8, out_ref.shape[1]), BF16)
    block = jnp.concatenate([sums_b[0:3, :], sums_a[0:3, :], shift, fields], axis=0).astype(BF16)
    out_ref[rows:, :] = jnp.concatenate([block, zero], axis=0)


def far_attention_grads(
    side_ref, x_ref, grad_out_ref, a2_ref, b2_ref, a3_ref, b3_ref, order_ref, turned_ref, fields_ref, probs_ref, ctx_ref,
    sums_b_ref, sums_a_ref, shift_ref, g3_ref, g2_ref, sum_ref, w_ref, tok_ref,
):
    tokens, grad_out = x_ref[...], grad_out_ref[...]
    total = None
    for group, a_ref, b_ref, out_ref in ((1, a3_ref, b3_ref, g3_ref), (0, a2_ref, b2_ref, g2_ref)):
        assemble(w_ref, a_ref, b_ref, side_ref[0])
        part, sums = attend_back(
            tokens, grad_out, w_ref, order_ref, turned_ref, group, fields_ref, probs_ref, ctx_ref, out_ref, tok_ref
        )
        put_vectors(out_ref, tokens.shape[1], sums_b_ref[...], sums_a_ref[...], shift_ref[group : group + 1, :], sums)
        total = part if total is None else total + part
    sum_ref[...] = total


def near_attention_grads(
    x_ref, grad_out_ref, w0_ref, w1_ref, order_ref, turned_ref, fields_ref, probs_ref, ctx_ref,
    sums_b_ref, sums_a_ref, shift_ref, sum_ref, grad_a_ref, g1_ref, g0_ref, in_ref, tok_ref,
):
    tokens, grad_out = x_ref[...], grad_out_ref[...]
    total = sum_ref[...] + grad_a_ref[...]
    for group, w_ref, out_ref in ((1, w1_ref, g1_ref), (0, w0_ref, g0_ref)):
        part, sums = attend_back(
            tokens, grad_out, w_ref, order_ref, turned_ref, group, fields_ref, probs_ref, ctx_ref, out_ref, tok_ref
        )
        put_vectors(out_ref, tokens.shape[1], sums_b_ref[...], sums_a_ref[...], shift_ref[group : group + 1, :], sums)
        total = total + part
    in_ref[...] = total.astype(BF16)


def solution(mesh):
    dp_size, tensor_size = mesh.shape["dp"], mesh.shape["tensor"]
    levels = dp_size.bit_length() - 1

    def swap(v, axis, bit):
        size = tensor_size if axis == "tensor" else dp_size
        return lax.ppermute(v, axis, [(i, i ^ (1 << bit)) for i in range(size)])

    def core_swap(v):
        return swap(v, "tensor", 0)

    def chip_swap(v):
        return swap(v, "tensor", 1)

    def add(a, b):
        return lax.reduce_precision(a.astype(F32) + b.astype(F32), 8, 7).astype(BF16)

    def on_device(
        layer_input, out_cotangent, qkv_weight, qv_bias, out_weight, out_bias, norm1_gain, norm1_bias,
        up_weight, up_bias, down_weight, down_bias, norm2_gain, norm2_bias, cluster_perm, segment_ids,
    ):
        length, width = layer_input.shape
        seqs, heads, _ = cluster_perm.shape
        units = up_weight.shape[1]
        mine = lax.axis_index("tensor")
        place = lax.axis_index("dp")
        side = place & 1
        half = width // 2
        side_arg = side.reshape(1).astype(jnp.int32)

        packed = call(pack_kernel, [((width, heads * SLOT), BF16)], [], 0, qkv_weight, out_weight)[0]
        head_bias = jnp.stack(
            [qv_bias[0].reshape(heads, HEAD_DIM), jnp.zeros((heads, HEAD_DIM), BF16), qv_bias[1].reshape(heads, HEAD_DIM),
             jnp.zeros((heads, HEAD_DIM), BF16)], axis=1
        ).reshape(heads * SLOT)

        def lined(v):
            wide = -(-v.shape[0] // length) * length
            return jnp.pad(v.astype(F32), (0, wide - v.shape[0])).reshape(-1, length)

        small = jnp.concatenate(
            [cluster_perm.reshape(seqs * heads, length).astype(F32), lined(up_bias), lined(head_bias)], axis=0
        )
        up_rows = -(-units // length)

        def own_half(m):
            return lax.dynamic_slice_in_dim(m, side * half, half, axis=0)

        small_1 = core_swap(small)
        small_2 = chip_swap(small)
        small_3 = core_swap(small_2)

        def gather(m):
            first = chip_swap(own_half(m))
            second = swap(first, "dp", 0)
            return core_swap(m), (first, second, core_swap(first), core_swap(second))

        c1, c_far = gather(packed)
        u1, u_far = gather(up_weight)
        d1, d_far = gather(down_weight)

        seg = lax.dynamic_slice_in_dim(segment_ids, mine, 1, axis=0).astype(F32)

        def orders(*packs):
            rows = [lax.dynamic_slice_in_dim(p, mine * heads, heads, axis=0) for p in packs]
            table = jnp.concatenate(rows + [seg, jnp.zeros((1, length), F32)], axis=0)
            at = seqs * heads
            shift = jnp.stack([p[at : at + up_rows].reshape(-1)[:units] for p in packs])
            bias = jnp.concatenate([p[at + up_rows :].reshape(-1)[: heads * SLOT].reshape(heads, SLOT) for p in packs])
            return table, table.T, shift, bias

        near_order, near_turned, near_shift, near_bias = orders(small, small_1)
        far_order, far_turned, far_shift, far_bias = orders(small_2, small_3)
        zero = jnp.zeros_like(out_bias)
        vecs = jnp.stack(
            [out_bias, norm1_gain, norm1_bias, down_bias, norm2_gain, norm2_bias, zero, zero]
        ).astype(F32)

        big = length * width * width * 2
        fields_t = ((2 * heads, length, SLOT), BF16)
        probs_t = ((2 * heads, length, CLUSTER), BF16)
        ctx_t = ((2, length, heads * HEAD_DIM), BF16)
        rows_f, rows_b = ((length, width), F32), ((length, width), BF16)
        pair_b = ((2, length, units), BF16)
        square = ((width, width), BF16)
        tall = ((width + EXTRA, heads * SLOT), BF16)
        vec_t = ((8, width), F32)
        mat = pltpu.VMEM((width, width), BF16)

        near_fields, near_probs, near_ctx, attn_sum = call(
            near_attention, [fields_t, probs_t, ctx_t, rows_f], [], 4 * big,
            layer_input, packed, c1, near_bias, near_order, near_turned,
        )
        far_fields, far_probs, far_ctx, low, normed_a, inverse_a = call(
            far_attention, [fields_t, probs_t, ctx_t, rows_b, rows_f, ((length, 1), F32)],
            [pltpu.VMEM((2, width, width), BF16)], 4 * big,
            side_arg, layer_input, *c_far, far_bias, far_order, far_turned, attn_sum, vecs,
        )
        near_hidden, near_slope, ffn_sum = call(
            near_forward, [pair_b, pair_b, rows_f], [], 4 * big, low, up_weight, u1, down_weight, d1, near_shift
        )
        far_hidden, far_slope = call(
            far_up, [pair_b, pair_b], [mat], 3 * big, side_arg, low, *u_far, far_shift
        )
        layer_output, grad_b, grad_b_low, sums_b = call(
            far_down, [rows_b, rows_f, rows_b, vec_t], [mat], 3 * big,
            side_arg, far_hidden, *d_far, ffn_sum, normed_a, out_cotangent, vecs,
        )
        dg3, dg2 = call(down_grads, [square, square], [], 2 * big, far_hidden, grad_b_low)
        dg1, dg0 = call(down_grads, [square, square], [], 2 * big, near_hidden, grad_b_low)
        ug3, ug2, grad_mid, far_ub = call(
            far_up_grads, [square, square, rows_f, vec_t], [mat, mat], 6 * big,
            side_arg, grad_b_low, low, far_slope, *d_far, *u_far,
        )
        ug1, ug0, grad_a, grad_a_low, near_ub, sums_a = call(
            near_up_grads, [square, square, rows_f, rows_b, vec_t, vec_t], [], 6 * big,
            grad_b_low, low, near_slope, down_weight, d1, up_weight, u1, grad_mid, grad_b, normed_a, inverse_a, vecs,
        )
        cg3, cg2, in_sum = call(
            far_attention_grads, [tall, tall, rows_f], [mat, pltpu.VMEM((length, width), BF16)], 6 * big,
            side_arg, layer_input, grad_a_low, *c_far, far_order, far_turned, far_fields, far_probs, far_ctx,
            sums_b, sums_a, far_ub,
        )
        cg1, cg0, input_grad = call(
            near_attention_grads, [tall, tall, rows_b], [pltpu.VMEM((length, width), BF16)], 6 * big,
            layer_input, grad_a_low, packed, c1, near_order, near_turned, near_fields, near_probs, near_ctx,
            sums_b, sums_a, near_ub, in_sum, grad_a,
        )

        def reduce(g3, g2, g1, g0):
            crossing = add(g2, core_swap(g3))
            total = add(add(g0, core_swap(g1)), chip_swap(crossing))
            for level in range(levels):
                rows = total.shape[0] // 2
                bit = (place >> level) & 1
                send = lax.dynamic_slice_in_dim(total, (1 - bit) * rows, rows, axis=0)
                keep = lax.dynamic_slice_in_dim(total, bit * rows, rows, axis=0)
                total = add(keep, swap(send, "dp", level))
            for level in reversed(range(levels)):
                bit = (place >> level) & 1
                other = swap(total, "dp", level)
                total = jnp.where(
                    bit == 0, jnp.concatenate([total, other], axis=0), jnp.concatenate([other, total], axis=0)
                )
            return total

        down_grad = reduce(dg3, dg2, dg1, dg0).astype(F32)
        up_grad = reduce(ug3, ug2, ug1, ug0).astype(F32)
        packed_grad = reduce(cg3, cg2, cg1, cg0)
        qkv_grad, out_grad, sums = call(
            unpack_kernel,
            [((3, width, heads * HEAD_DIM), F32), ((heads * HEAD_DIM, width), F32), ((16, width), F32)], [], 0,
            packed_grad,
        )
        field_sums = sums[7].reshape(heads, 4, HEAD_DIM)
        qv_grad = jnp.stack([field_sums[:, 0].reshape(-1), field_sums[:, 2].reshape(-1)])
        return (
            layer_output, input_grad, qkv_grad, qv_grad, out_grad, sums[5], sums[3], sums[4],
            up_grad, sums[6], down_grad, sums[2], sums[0], sums[1],
        )

    rows, split, copied = P(("dp", "tensor"), None), P(None, "tensor"), P()
    in_specs = (
        rows, rows, P(None, None, "tensor"), split, P("tensor", None), copied, copied, copied, split, P("tensor"),
        P("tensor", None), copied, copied, copied, P("dp", "tensor", None), P("dp", None),
    )
    out_specs = (
        rows, rows, P(None, None, "tensor"), split, P("tensor", None), copied, copied, copied, split, P("tensor"),
        P("tensor", None), copied, copied, copied,
    )
    return jax.shard_map(on_device, mesh=mesh, in_specs=in_specs, out_specs=out_specs, check_vma=False)
```

```python
import math

import jax
import jax.numpy as jnp
from jax import lax
from jax.experimental import pallas as pl
from jax.experimental.pallas import tpu as pltpu
from jax.sharding import PartitionSpec as P

HEAD_DIM = 64
CLUSTER = 128
NORM_EPS = 1e-12
MASKED = -1000000000.0
ROOT_HALF = 0.7071067811865476
INV_ROOT_TWO_PI = 0.3989422804014327
SCALE = 1.0 / math.sqrt(HEAD_DIM)
SLOT = 4 * HEAD_DIM
PAIR = 2 * HEAD_DIM
BLOCK = 128
VMEM_LIMIT = 30 * 1024 * 1024
EXTRA = 64
F32 = jnp.float32
BF16 = jnp.bfloat16


def mm(a, b):
    return jnp.dot(a, b, preferred_element_type=F32)


def mm_nt(a, b):
    return lax.dot_general(a, b, (((1,), (1,)), ((), ())), preferred_element_type=F32)


def mm_tn(a, b):
    return lax.dot_general(a, b, (((0,), (0,)), ((), ())), preferred_element_type=F32)


def call(body, outs, scratch, micros, *args, after=()):
    shapes = [jax.ShapeDtypeStruct(s, t) for s, t in outs]
    kept = len(args)

    def placed(a):
        flat = a.ndim == 1 and a.dtype == jnp.int32
        return pl.BlockSpec(memory_space=pltpu.SMEM if flat else pltpu.VMEM)

    def run(*refs):
        body(*refs[:kept], *refs[kept + len(after) :])

    return pl.pallas_call(
        run,
        out_shape=shapes,
        in_specs=[placed(a) for a in args] + [pl.BlockSpec(memory_space=pl.ANY)] * len(after),
        out_specs=[pl.BlockSpec(memory_space=pltpu.VMEM)] * len(outs),
        scratch_shapes=scratch,
        cost_estimate=pl.CostEstimate(flops=int(micros * 1e9), bytes_accessed=0, transcendentals=0),
        compiler_params=pltpu.CompilerParams(vmem_limit_bytes=VMEM_LIMIT),
    )(*args, *after)


def tie(value, *others):
    return lax.optimization_barrier((value, *others))[0]


def norm(values):
    center = values - jnp.mean(values, axis=-1, keepdims=True)
    inverse = lax.rsqrt(jnp.mean(center * center, axis=-1, keepdims=True) + NORM_EPS)
    return center * inverse, inverse


def norm_back(grad_in, normed, inverse, gain):
    scaled = grad_in * gain
    return inverse * (
        scaled
        - jnp.mean(scaled, axis=-1, keepdims=True)
        - normed * jnp.mean(scaled * normed, axis=-1, keepdims=True)
    )


def colsum(v):
    return jnp.sum(v, axis=0, keepdims=True)


def assemble(scratch, half_ref, relayed_ref, side):
    rows = half_ref.shape[0]
    here, there = half_ref[...], relayed_ref[...]
    scratch[0:rows, :] = jnp.where(side == 0, here, there)
    scratch[rows : 2 * rows, :] = jnp.where(side == 0, there, here)


def prepare(where_ref, qkv_ref, out_ref, perm_ref, vec_ref, packed_ref, half_ref, small_ref, lines_ref):
    width = qkv_ref.shape[1]
    turned = out_ref[...].astype(F32).T.astype(BF16)
    heads = qkv_ref.shape[2] // HEAD_DIM
    for h in range(heads):
        cut = slice(h * HEAD_DIM, (h + 1) * HEAD_DIM)
        packed_ref[:, h * SLOT : (h + 1) * SLOT] = jnp.concatenate(
            [qkv_ref[0, :, cut], qkv_ref[2, :, cut], qkv_ref[1, :, cut], turned[:, cut]], axis=1
        )
    half = width // 2
    half_ref[...] = jnp.where(where_ref[0] == 0, packed_ref[0:half, :], packed_ref[half:width, :])
    lines = vec_ref[...].astype(F32)
    lines_ref[...] = lines
    seqs = perm_ref.shape[0]
    for s in range(seqs):
        small_ref[s * heads : (s + 1) * heads, :] = perm_ref[s].astype(F32)
    own = heads * HEAD_DIM
    blank = jnp.zeros((1, 2 * HEAD_DIM), F32)
    bias = []
    for h in range(heads):
        bias += [lines[7:8, h * HEAD_DIM : (h + 1) * HEAD_DIM], lines[7:8, own + h * HEAD_DIM : own + (h + 1) * HEAD_DIM], blank]
    length = small_ref.shape[1]
    for row, line in ((seqs * heads, lines[6:7, :]), (seqs * heads + 2, jnp.concatenate(bias, axis=1))):
        small_ref[row : row + 1, :] = line[:, 0:length]
        rest = line.shape[1] - length
        small_ref[row + 1 : row + 2, :] = jnp.concatenate([line[:, length:], jnp.zeros((1, length - rest), F32)], axis=1)


def unpack(packed_ref, qkv_ref, out_ref, vec_ref):
    width = packed_ref.shape[1]
    heads = width // SLOT
    rows = qkv_ref.shape[1]

    def field(at):
        return jnp.concatenate(
            [packed_ref[0:rows, h * SLOT + at * HEAD_DIM : h * SLOT + (at + 1) * HEAD_DIM] for h in range(heads)], axis=1
        ).astype(F32)

    qkv_ref[0], qkv_ref[2], qkv_ref[1] = field(0), field(1), field(2)
    out_ref[...] = field(3).T
    vec_ref[...] = packed_ref[rows : rows + 16, :].astype(F32)


def put_orders(where_ref, packs, seg_ref, order_ref, turned_ref):
    heads = order_ref.shape[0] // 2 - 1
    order_ref[...] = jnp.zeros_like(order_ref)
    for group, pack in enumerate(packs):
        for h in range(heads):
            at = group * heads + h
            order_ref[at : at + 1, :] = pack[pl.ds(where_ref[1] * heads + h, 1), :]
    order_ref[2 * heads : 2 * heads + 1, :] = seg_ref[pl.ds(where_ref[1], 1), :].astype(F32)
    turned_ref[...] = order_ref[...].T


def put_tables(order_ref, turned_ref, count, place_ref, position_ref):
    length = order_ref.shape[1]
    lane = lax.broadcasted_iota(jnp.int32, (length, length), 1).astype(F32)
    sub = lax.broadcasted_iota(jnp.int32, (length, length), 0).astype(F32)
    for at in range(count):
        place_ref[at] = jnp.where(turned_ref[:, at : at + 1] == lane, 1.0, 0.0).astype(BF16)
        position_ref[at] = jnp.where(order_ref[at : at + 1, :] == sub, 1.0, 0.0).astype(BF16)


def put_out_columns(weights, columns_ref):
    heads = weights[0].shape[1] // SLOT
    for group, w_ref in enumerate(weights):
        for h in range(heads):
            at = group * heads + h
            columns_ref[:, at * PAIR : (at + 1) * PAIR] = w_ref[:, h * SLOT + PAIR : (h + 1) * SLOT]


def cuts(length):
    return [slice(c, c + CLUSTER) for c in range(0, length, CLUSTER)]


def attend(
    x_ref, weights, packs, order_ref, turned_ref, fields_ref, probs_ref, ctx_ref,
    place_ref, position_ref, raw_ref, scores_ref, columns_ref,
):
    length = x_ref.shape[0]
    heads = weights[0].shape[1] // SLOT
    count = 2 * heads
    lanes = lax.broadcasted_iota(jnp.int32, (length, SLOT), 1)
    bias_row = packs[0].shape[0] - 2
    for group, (w_ref, pack) in enumerate(zip(weights, packs)):
        bias = jnp.concatenate([pack[bias_row : bias_row + 1, :], pack[bias_row + 1 : bias_row + 2, :]], axis=1)
        for h in range(heads):
            fields = mm(x_ref[...], w_ref[:, h * SLOT : (h + 1) * SLOT]) + bias[:, h * SLOT : (h + 1) * SLOT]
            raw_ref[group * heads + h] = jnp.where(lanes < 3 * HEAD_DIM, fields, turned_ref[:, count : count + 1]).astype(BF16)
    put_tables(order_ref, turned_ref, count, place_ref, position_ref)
    order_low = order_ref[...].astype(BF16)
    seg_rows = []
    for at in range(count):
        fields_ref[at] = mm(place_ref[at], raw_ref[at]).astype(BF16)
        seg_rows.append(mm(order_low, position_ref[at])[count : count + 1, :])
    for at in range(count):
        for c, cut in enumerate(cuts(length)):
            seg_col = fields_ref[at, cut, SLOT - PAIR : SLOT].astype(F32)[:, PAIR - 1 : PAIR]
            scores = mm_nt(fields_ref[at, cut, 0:HEAD_DIM], fields_ref[at, cut, PAIR : PAIR + HEAD_DIM]) * SCALE
            scores_ref[at, cut, :] = jnp.where(seg_col == seg_rows[at][:, cut], scores, MASKED)
    for at in range(count):
        for cut in cuts(length):
            scores = scores_ref[at, cut, :]
            raised = jnp.exp(scores - jnp.max(scores, axis=-1, keepdims=True))
            probs_ref[at, cut, :] = (raised / jnp.sum(raised, axis=-1, keepdims=True)).astype(BF16)
    low_lanes = lax.broadcasted_iota(jnp.int32, (CLUSTER, PAIR), 1) < HEAD_DIM
    for at in range(count):
        for cut in cuts(length):
            mixed = mm(probs_ref[at, cut, :], fields_ref[at, cut, 0:PAIR])
            raw_ref[at, cut, 0:PAIR] = jnp.where(low_lanes, 0.0, mixed).astype(BF16)
    for at in range(count):
        ctx_ref[:, at * PAIR : (at + 1) * PAIR] = mm(position_ref[at], raw_ref[at, :, 0:PAIR]).astype(BF16)
    put_out_columns(weights, columns_ref)


def near_attention(
    where_ref, x_ref, w0_ref, w1_ref, pack0_ref, pack1_ref, seg_ref,
    fields_ref, probs_ref, ctx_ref, sum_ref, order_ref, turned_ref,
    place_ref, position_ref, raw_ref, scores_ref, columns_ref,
):
    packs = (pack0_ref, pack1_ref)
    put_orders(where_ref, packs, seg_ref, order_ref, turned_ref)
    attend(
        x_ref, (w0_ref, w1_ref), packs, order_ref, turned_ref, fields_ref, probs_ref, ctx_ref,
        place_ref, position_ref, raw_ref, scores_ref, columns_ref,
    )
    sum_ref[...] = mm_nt(ctx_ref[...], columns_ref[...])


def blocks(length):
    return [slice(r, r + BLOCK) for r in range(0, length, BLOCK)]


def far_attention(
    where_ref, x_ref, a2_ref, b2_ref, a3_ref, b3_ref, pack2_ref, pack3_ref, seg_ref, sum_ref, vec_ref,
    fields_ref, probs_ref, ctx_ref, order_ref, turned_ref, low_ref, normed_ref, inverse_ref,
    place_ref, position_ref, raw_ref, scores_ref, columns_ref, w2_ref, w3_ref, total_ref,
):
    packs = (pack2_ref, pack3_ref)
    assemble(w2_ref, a2_ref, b2_ref, where_ref[0])
    assemble(w3_ref, a3_ref, b3_ref, where_ref[0])
    put_orders(where_ref, packs, seg_ref, order_ref, turned_ref)
    attend(
        x_ref, (w2_ref, w3_ref), packs, order_ref, turned_ref, fields_ref, probs_ref, ctx_ref,
        place_ref, position_ref, raw_ref, scores_ref, columns_ref,
    )
    total_ref[...] = mm_nt(ctx_ref[...], columns_ref[...])
    for r in blocks(x_ref.shape[0]):
        normed, inverse = norm(x_ref[r, :].astype(F32) + sum_ref[r, :] + total_ref[r, :] + vec_ref[0:1, :])
        low_ref[r, :] = (normed * vec_ref[1:2, :] + vec_ref[2:3, :]).astype(BF16)
        normed_ref[r, :] = normed
        inverse_ref[r, :] = inverse


def up_bias(pack_ref, width):
    row = pack_ref.shape[0] - 4
    return jnp.concatenate([pack_ref[row : row + 1, :], pack_ref[row + 1 : row + 2, :]], axis=1)[:, 0:width]


def hidden_units(low_ref, up_ref, shift, hidden_ref, slope_ref):
    length = low_ref.shape[0]
    for r in blocks(length):
        v = mm(low_ref[r, :], up_ref[...]) + shift
        half = 0.5 + 0.5 * lax.erf(v * ROOT_HALF)
        hidden_ref[r, :] = (v * half).astype(BF16)
        slope_ref[r, :] = (half + v * jnp.exp(-0.5 * v * v) * INV_ROOT_TWO_PI).astype(BF16)


def near_forward(low_ref, u0_ref, u1_ref, d0_ref, d1_ref, pack0_ref, pack1_ref, hidden_ref, slope_ref, sum_ref):
    width = u0_ref.shape[1]
    hidden_units(low_ref, u0_ref, up_bias(pack0_ref, width), hidden_ref.at[0], slope_ref.at[0])
    hidden_units(low_ref, u1_ref, up_bias(pack1_ref, width), hidden_ref.at[1], slope_ref.at[1])
    for r in blocks(low_ref.shape[0]):
        sum_ref[r, :] = mm(hidden_ref[0, r, :], d0_ref[...]) + mm(hidden_ref[1, r, :], d1_ref[...])


def far_up(where_ref, low_ref, a2_ref, b2_ref, a3_ref, b3_ref, pack2_ref, pack3_ref, hidden_ref, slope_ref, u2_ref, u3_ref):
    width = a2_ref.shape[1]
    assemble(u2_ref, a2_ref, b2_ref, where_ref[0])
    assemble(u3_ref, a3_ref, b3_ref, where_ref[0])
    hidden_units(low_ref, u2_ref, up_bias(pack2_ref, width), hidden_ref.at[0], slope_ref.at[0])
    hidden_units(low_ref, u3_ref, up_bias(pack3_ref, width), hidden_ref.at[1], slope_ref.at[1])


def far_down(
    where_ref, hidden_ref, a2_ref, b2_ref, a3_ref, b3_ref, sum_ref, normed_a_ref, cot_ref, vec_ref,
    out_ref, grad_ref, grad_low_ref, sums_ref, d2_ref, d3_ref,
):
    assemble(d2_ref, a2_ref, b2_ref, where_ref[0])
    assemble(d3_ref, a3_ref, b3_ref, where_ref[0])
    sums_ref[...] = jnp.zeros_like(sums_ref)
    for r in blocks(hidden_ref.shape[1]):
        total = sum_ref[r, :] + mm(hidden_ref[0, r, :], d2_ref[...]) + mm(hidden_ref[1, r, :], d3_ref[...])
        middle = normed_a_ref[r, :] * vec_ref[1:2, :] + vec_ref[2:3, :]
        normed, inverse = norm(middle + total + vec_ref[3:4, :])
        out_ref[r, :] = (normed * vec_ref[4:5, :] + vec_ref[5:6, :]).astype(BF16)
        cot = cot_ref[r, :].astype(F32)
        grad = norm_back(cot, normed, inverse, vec_ref[4:5, :])
        grad_ref[r, :] = grad
        grad_low_ref[r, :] = grad.astype(BF16)
        sums_ref[0:1, :] += colsum(cot * normed)
        sums_ref[1:2, :] += colsum(cot)
        sums_ref[2:3, :] += colsum(grad)


def down_grads(far_ref, near_ref, grad_low_ref, g3_ref, g2_ref, g1_ref, g0_ref):
    g3_ref[...] = mm_tn(far_ref[1], grad_low_ref[...]).astype(BF16)
    g2_ref[...] = mm_tn(far_ref[0], grad_low_ref[...]).astype(BF16)
    g1_ref[...] = mm_tn(near_ref[1], grad_low_ref[...]).astype(BF16)
    g0_ref[...] = mm_tn(near_ref[0], grad_low_ref[...]).astype(BF16)


def up_grads(grad_low_ref, low_ref, slope_ref, down_ref, up_ref, pre_ref, out_ref, mid_ref, first, sums_ref, at):
    pre = (mm_nt(grad_low_ref[...], down_ref[...]) * slope_ref[...].astype(F32)).astype(BF16)
    pre_ref[...] = pre
    sums_ref[at : at + 1, :] = colsum(pre.astype(F32))
    out_ref[...] = mm_tn(low_ref[...], pre_ref[...]).astype(BF16)
    part = mm_nt(pre_ref[...], up_ref[...])
    mid_ref[...] = part if first else mid_ref[...] + part


def far_up_grads(
    where_ref, grad_low_ref, low_ref, slope_ref, d2a_ref, d2b_ref, d3a_ref, d3b_ref, u2a_ref, u2b_ref, u3a_ref, u3b_ref,
    g3_ref, g2_ref, mid_ref, shift_ref, d2_ref, d3_ref, u2_ref, u3_ref, pre2_ref, pre3_ref,
):
    side = where_ref[0]
    shift_ref[...] = jnp.zeros_like(shift_ref)
    assemble(d3_ref, d3a_ref, d3b_ref, side)
    assemble(u3_ref, u3a_ref, u3b_ref, side)
    assemble(d2_ref, d2a_ref, d2b_ref, side)
    assemble(u2_ref, u2a_ref, u2b_ref, side)
    up_grads(grad_low_ref, low_ref, slope_ref.at[1], d3_ref, u3_ref, pre3_ref, g3_ref, mid_ref, True, shift_ref, 1)
    up_grads(grad_low_ref, low_ref, slope_ref.at[0], d2_ref, u2_ref, pre2_ref, g2_ref, mid_ref, False, shift_ref, 0)


def near_up_grads(
    grad_low_ref, low_ref, slope_ref, d0_ref, d1_ref, u0_ref, u1_ref, far_mid_ref, grad_b_ref, normed_ref, inverse_ref,
    vec_ref, g1_ref, g0_ref, grad_ref, grad_out_ref, shift_ref, sums_ref, pre0_ref, pre1_ref, mid_ref,
):
    shift_ref[...] = jnp.zeros_like(shift_ref)
    sums_ref[...] = jnp.zeros_like(sums_ref)
    up_grads(grad_low_ref, low_ref, slope_ref.at[1], d1_ref, u1_ref, pre1_ref, g1_ref, mid_ref, True, shift_ref, 1)
    up_grads(grad_low_ref, low_ref, slope_ref.at[0], d0_ref, u0_ref, pre0_ref, g0_ref, mid_ref, False, shift_ref, 0)
    for r in blocks(low_ref.shape[0]):
        total = mid_ref[r, :] + far_mid_ref[r, :] + grad_b_ref[r, :]
        normed = normed_ref[r, :]
        grad = norm_back(total, normed, inverse_ref[r, :], vec_ref[1:2, :])
        grad_ref[r, :] = grad
        grad_out_ref[r, :] = grad.astype(BF16)
        sums_ref[0:1, :] += colsum(total * normed)
        sums_ref[1:2, :] += colsum(total)
        sums_ref[2:3, :] += colsum(grad)


def attend_back(
    x_ref, grad_out_ref, weights, order_ref, turned_ref, fields_ref, probs_ref, ctx_ref, outs,
    sums_b_ref, sums_a_ref, shift_ref, place_ref, position_ref, columns_ref, grads_ref, moved_ref, raw_ref, tok_ref, scores_ref, low_ref,
):
    length, width = x_ref.shape
    heads = weights[0].shape[1] // SLOT
    count = 2 * heads
    put_tables(order_ref, turned_ref, count, place_ref, position_ref)
    put_out_columns(weights, columns_ref)
    grads_ref[...] = mm(grad_out_ref[...], columns_ref[...]).astype(BF16)
    for at in range(count):
        moved_ref[at] = mm(place_ref[at], grads_ref[:, at * PAIR : (at + 1) * PAIR]).astype(BF16)
    low_lanes = lax.broadcasted_iota(jnp.int32, (CLUSTER, PAIR), 1) < HEAD_DIM
    no_low = jnp.zeros((CLUSTER, PAIR), BF16)
    for at in range(count):
        for cut in cuts(length):
            values = jnp.where(low_lanes, no_low, fields_ref[at, cut, 0:PAIR])
            scores_ref[at, cut, :] = mm_nt(moved_ref[at, cut, :], values)
    for at in range(count):
        for cut in cuts(length):
            grad_probs = scores_ref[at, cut, :]
            probs = probs_ref[at, cut, :].astype(F32)
            delta = jnp.sum(grad_probs * probs, axis=-1, keepdims=True)
            low_ref[at, cut, :] = (probs * (grad_probs - delta)).astype(BF16)
    for at in range(count):
        for cut in cuts(length):
            grad_queries = mm(low_ref[at, cut, :], fields_ref[at, cut, PAIR:SLOT]) * SCALE
            grad_values = mm_tn(probs_ref[at, cut, :], moved_ref[at, cut, :])
            raw_ref[at, cut, 0:PAIR] = jnp.where(low_lanes, grad_queries, grad_values).astype(BF16)
    for at in range(count):
        for cut in cuts(length):
            grad_keys = mm_tn(low_ref[at, cut, :], fields_ref[at, cut, 0:PAIR]) * SCALE
            raw_ref[at, cut, PAIR:SLOT] = jnp.where(low_lanes, grad_keys, 0.0).astype(BF16)
    for group, out_ref in reversed(list(enumerate(outs))):
        for h in range(heads):
            at = group * heads + h
            tok_ref[group, :, h * SLOT : (h + 1) * SLOT] = mm(position_ref[at], raw_ref[at]).astype(BF16)
        out_grad = mm_tn(grad_out_ref[...], ctx_ref[:, group * heads * PAIR : (group + 1) * heads * PAIR])
        grad = mm_tn(x_ref[...], tok_ref[group])
        for h in range(heads):
            out_ref[0:width, h * SLOT : h * SLOT + PAIR] = grad[:, h * SLOT : h * SLOT + PAIR].astype(BF16)
            out_ref[0:width, h * SLOT + PAIR : (h + 1) * SLOT] = (
                grad[:, h * SLOT + PAIR : (h + 1) * SLOT] + out_grad[:, h * PAIR : (h + 1) * PAIR]
            ).astype(BF16)
        fields = colsum(tok_ref[group].astype(F32))
        block = jnp.concatenate([sums_b_ref[0:3, :], sums_a_ref[0:3, :], shift_ref[group : group + 1, :], fields], axis=0)
        zero = jnp.zeros((EXTRA - 8, width), F32)
        out_ref[width:, :] = jnp.concatenate([block, zero], axis=0).astype(BF16)


def far_attention_grads(
    where_ref, x_ref, grad_out_ref, a2_ref, b2_ref, a3_ref, b3_ref, order_ref, turned_ref, fields_ref, probs_ref, ctx_ref,
    sums_b_ref, sums_a_ref, shift_ref, g3_ref, g2_ref, sum_ref,
    place_ref, position_ref, columns_ref, grads_ref, moved_ref, raw_ref, tok_ref, scores_ref, low_ref, w2_ref, w3_ref,
):
    assemble(w2_ref, a2_ref, b2_ref, where_ref[0])
    assemble(w3_ref, a3_ref, b3_ref, where_ref[0])
    attend_back(
        x_ref, grad_out_ref, (w2_ref, w3_ref), order_ref, turned_ref, fields_ref, probs_ref, ctx_ref, (g2_ref, g3_ref),
        sums_b_ref, sums_a_ref, shift_ref, place_ref, position_ref, columns_ref, grads_ref, moved_ref, raw_ref, tok_ref, scores_ref, low_ref,
    )
    sum_ref[...] = mm_nt(tok_ref[0], w2_ref[...]) + mm_nt(tok_ref[1], w3_ref[...])


def near_attention_grads(
    x_ref, grad_out_ref, w0_ref, w1_ref, order_ref, turned_ref, fields_ref, probs_ref, ctx_ref,
    sums_b_ref, sums_a_ref, shift_ref, sum_ref, grad_a_ref, g1_ref, g0_ref, in_ref,
    place_ref, position_ref, columns_ref, grads_ref, moved_ref, raw_ref, tok_ref, scores_ref, low_ref,
):
    attend_back(
        x_ref, grad_out_ref, (w0_ref, w1_ref), order_ref, turned_ref, fields_ref, probs_ref, ctx_ref, (g0_ref, g1_ref),
        sums_b_ref, sums_a_ref, shift_ref, place_ref, position_ref, columns_ref, grads_ref, moved_ref, raw_ref, tok_ref, scores_ref, low_ref,
    )
    in_ref[...] = (mm_nt(tok_ref[0], w0_ref[...]) + mm_nt(tok_ref[1], w1_ref[...]) + sum_ref[...] + grad_a_ref[...]).astype(BF16)


def solution(mesh):
    dp_size, tensor_size = mesh.shape["dp"], mesh.shape["tensor"]
    levels = dp_size.bit_length() - 1

    def swap(v, axis, bit):
        size = tensor_size if axis == "tensor" else dp_size
        return lax.ppermute(v, axis, [(i, i ^ (1 << bit)) for i in range(size)])

    def core_swap(v):
        return swap(v, "tensor", 0)

    def chip_swap(v):
        return swap(v, "tensor", 1)

    def add(a, b):
        return lax.reduce_precision(a.astype(F32) + b.astype(F32), 8, 7).astype(BF16)

    def on_device(
        layer_input, out_cotangent, qkv_weight, qv_bias, out_weight, out_bias, norm1_gain, norm1_bias,
        up_weight, up_bias, down_weight, down_bias, norm2_gain, norm2_bias, cluster_perm, segment_ids,
    ):
        length, width = layer_input.shape
        seqs, heads, _ = cluster_perm.shape
        units = up_weight.shape[1]
        mine = lax.axis_index("tensor")
        place = lax.axis_index("dp")
        side = place & 1
        half = width // 2

        where_arg = jnp.stack([side, mine]).astype(jnp.int32)
        count = 2 * heads
        lines = jnp.concatenate(
            [out_bias, norm1_gain, norm1_bias, down_bias, norm2_gain, norm2_bias, up_bias, qv_bias.reshape(-1),
             jnp.zeros((2 * width - units - 2 * heads * HEAD_DIM,), BF16)]
        ).reshape(8, width)
        square, half_t = ((width, width), BF16), ((half, width), BF16)
        vec_t = ((8, width), F32)
        small_t = ((seqs * heads + 4, length), F32)
        packed, packed_half, small, vecs = call(
            prepare, [square, half_t, small_t, vec_t], [], 3, where_arg, qkv_weight, out_weight, cluster_perm, lines
        )

        def own_half(m):
            return lax.dynamic_slice_in_dim(m, side * half, half, axis=0)

        def gather(m, m_half):
            first = chip_swap(m_half)
            second = swap(first, "dp", 0)
            return core_swap(m), (first, second, core_swap(first), core_swap(second))

        small_2, small_1 = chip_swap(small), core_swap(small)
        halves = [packed_half, own_half(up_weight), own_half(down_weight)]
        c_first, u_first, d_first = [chip_swap(m) for m in halves]
        c1, u1, d1 = core_swap(packed), core_swap(up_weight), core_swap(down_weight)

        def relay(first):
            second = swap(first, "dp", 0)
            return first, second, core_swap(first), core_swap(second)

        fields_t = ((count, length, SLOT), BF16)
        probs_t = ((count, length, CLUSTER), BF16)
        ctx_t = ((length, count * PAIR), BF16)
        orders_t = [((8, length), F32), ((length, 8), F32)]
        rows_f, rows_b = ((length, width), F32), ((length, width), BF16)
        pair_b = ((2, length, units), BF16)
        tall = ((width + EXTRA, heads * SLOT), BF16)
        mat, rows_s = pltpu.VMEM((width, width), BF16), pltpu.VMEM((length, width), BF16)
        tables = [pltpu.VMEM((count, length, length), BF16)] * 2
        columns = pltpu.VMEM((width, count * PAIR), BF16)
        raw = pltpu.VMEM((count, length, SLOT), BF16)
        scores = pltpu.VMEM((count, length, CLUSTER), F32)
        back = tables + [columns, rows_s, pltpu.VMEM((count, length, PAIR), BF16), raw, pltpu.VMEM((2, length, width), BF16)]
        back += [scores, pltpu.VMEM((count, length, CLUSTER), BF16)]

        near_fields, near_probs, near_ctx, attn_sum, *near_orders = call(
            near_attention, [fields_t, probs_t, ctx_t, rows_f, *orders_t], [*tables, raw, scores, columns], 8,
            where_arg, layer_input, packed, c1, small, small_1, segment_ids, after=(small_2,),
        )
        small_3 = core_swap(tie(small_2, attn_sum))
        c_far = relay(tie(c_first, attn_sum))
        u_far = relay(tie(u_first, attn_sum))
        far_fields, far_probs, far_ctx, *far_orders, low, normed_a, inverse_a = call(
            far_attention, [fields_t, probs_t, ctx_t, *orders_t, rows_b, rows_f, ((length, 1), F32)],
            [*tables, raw, scores, columns, mat, mat, pltpu.VMEM((length, width), F32)], 9,
            where_arg, layer_input, *c_far, small_2, small_3, segment_ids, attn_sum, vecs,
        )
        d_far = relay(tie(d_first, low))
        near_hidden, near_slope, ffn_sum = call(
            near_forward, [pair_b, pair_b, rows_f], [], 6, low, up_weight, u1, down_weight, d1, small, small_1
        )
        far_hidden, far_slope = call(
            far_up, [pair_b, pair_b], [mat, mat], 5, where_arg, low, *u_far, small_2, small_3
        )
        layer_output, grad_b, grad_b_low, sums_b = call(
            far_down, [rows_b, rows_f, rows_b, vec_t], [mat, mat], 5,
            where_arg, far_hidden, *d_far, ffn_sum, normed_a, out_cotangent, vecs,
        )
        dg3, dg2, dg1, dg0 = call(down_grads, [square] * 4, [], 2.8, far_hidden, near_hidden, grad_b_low)
        ds3, ds1 = core_swap(dg3), core_swap(dg1)
        ug3, ug2, grad_mid, far_ub = call(
            far_up_grads, [square, square, rows_f, vec_t], [mat] * 4 + [rows_s] * 2, 0.1,
            where_arg, grad_b_low, low, far_slope, *d_far, *u_far,
        )
        us3 = core_swap(ug3)
        down_cross = add(dg2, tie(ds3, grad_mid))
        ug1, ug0, grad_a, grad_a_low, near_ub, sums_a = call(
            near_up_grads, [square, square, rows_f, rows_b, vec_t, vec_t], [rows_s, rows_s, pltpu.VMEM((length, width), F32)], 0.1,
            grad_b_low, low, near_slope, down_weight, d1, up_weight, u1, grad_mid, grad_b, normed_a, inverse_a, vecs,
            after=(down_cross,),
        )
        us1 = core_swap(ug1)
        up_cross = add(ug2, tie(us3, grad_a_low))
        cg3, cg2, in_sum = call(
            far_attention_grads, [tall, tall, rows_f], back + [mat, mat], 0.1,
            where_arg, layer_input, grad_a_low, *c_far, *far_orders, far_fields, far_probs, far_ctx, sums_b, sums_a, far_ub,
            after=(up_cross,),
        )
        cs3 = core_swap(cg3)
        down_total = add(add(dg0, ds1), tie(chip_swap(down_cross), in_sum))
        packed_cross = add(cg2, cs3)
        cg1, cg0, input_grad = call(
            near_attention_grads, [tall, tall, rows_b], back, 0.1,
            layer_input, grad_a_low, packed, c1, *near_orders, near_fields, near_probs, near_ctx,
            sums_b, sums_a, near_ub, in_sum, grad_a, after=(down_total, packed_cross),
        )
        up_total = add(add(ug0, us1), tie(chip_swap(up_cross), input_grad))
        packed_total = add(add(cg0, core_swap(cg1)), chip_swap(packed_cross))

        def reduce(total):
            for level in range(levels):
                rows = total.shape[0] // 2
                bit = (place >> level) & 1
                send = lax.dynamic_slice_in_dim(total, (1 - bit) * rows, rows, axis=0)
                keep = lax.dynamic_slice_in_dim(total, bit * rows, rows, axis=0)
                total = add(keep, swap(send, "dp", level))
            for level in reversed(range(levels)):
                bit = (place >> level) & 1
                other = swap(total, "dp", level)
                total = jnp.where(
                    bit == 0, jnp.concatenate([total, other], axis=0), jnp.concatenate([other, total], axis=0)
                )
            return total

        down_grad = reduce(down_total).astype(F32)
        up_grad = reduce(up_total).astype(F32)
        packed_grad = reduce(packed_total)
        qkv_grad, out_grad, sums = call(
            unpack,
            [((3, width, heads * HEAD_DIM), F32), ((heads * HEAD_DIM, width), F32), ((16, width), F32)], [], 1,
            packed_grad,
        )
        field_sums = sums[7].reshape(heads, 4, HEAD_DIM)
        qv_grad = jnp.stack([field_sums[:, 0].reshape(-1), field_sums[:, 1].reshape(-1)])
        return (
            layer_output, input_grad, qkv_grad, qv_grad, out_grad, sums[5], sums[3], sums[4],
            up_grad, sums[6], down_grad, sums[2], sums[0], sums[1],
        )

    rows, split, copied = P(("dp", "tensor"), None), P(None, "tensor"), P()
    in_specs = (
        rows, rows, P(None, None, "tensor"), split, P("tensor", None), copied, copied, copied, split, P("tensor"),
        P("tensor", None), copied, copied, copied, P("dp", "tensor", None), P("dp", None),
    )
    out_specs = (
        rows, rows, P(None, None, "tensor"), split, P("tensor", None), copied, copied, copied, split, P("tensor"),
        P("tensor", None), copied, copied, copied,
    )
    return jax.shard_map(on_device, mesh=mesh, in_specs=in_specs, out_specs=out_specs, check_vma=False)
```

```python
import math

import jax
import jax.numpy as jnp
from jax import lax
from jax.experimental import pallas as pl
from jax.experimental.pallas import tpu as pltpu
from jax.sharding import PartitionSpec as P

HEAD_DIM = 64
CLUSTER = 128
NORM_EPS = 1e-12
MASKED = -1000000000.0
ROOT_HALF = 0.7071067811865476
INV_ROOT_TWO_PI = 0.3989422804014327
SCALE = 1.0 / math.sqrt(HEAD_DIM)
SLOT = 4 * HEAD_DIM
PAIR = 2 * HEAD_DIM
BLOCK = 128
VMEM_LIMIT = 30 * 1024 * 1024
EXTRA = 64
F32 = jnp.float32
BF16 = jnp.bfloat16


def mm(a, b):
    return jnp.dot(a, b, preferred_element_type=F32)


def mm_nt(a, b):
    return lax.dot_general(a, b, (((1,), (1,)), ((), ())), preferred_element_type=F32)


def mm_tn(a, b):
    return lax.dot_general(a, b, (((0,), (0,)), ((), ())), preferred_element_type=F32)


def call(body, outs, scratch, micros, *args, after=()):
    shapes = [jax.ShapeDtypeStruct(s, t) for s, t in outs]
    kept = len(args)

    def placed(a):
        flat = a.ndim == 1 and a.dtype == jnp.int32
        return pl.BlockSpec(memory_space=pltpu.SMEM if flat else pltpu.VMEM)

    def run(*refs):
        body(*refs[:kept], *refs[kept + len(after) :])

    return pl.pallas_call(
        run,
        out_shape=shapes,
        in_specs=[placed(a) for a in args] + [pl.BlockSpec(memory_space=pl.ANY)] * len(after),
        out_specs=[pl.BlockSpec(memory_space=pltpu.VMEM)] * len(outs),
        scratch_shapes=scratch,
        cost_estimate=pl.CostEstimate(flops=int(micros * 1e9), bytes_accessed=0, transcendentals=0),
        compiler_params=pltpu.CompilerParams(vmem_limit_bytes=VMEM_LIMIT),
    )(*args, *after)


def tie(value, *others):
    return lax.optimization_barrier((value, *others))[0]


def norm(values):
    center = values - jnp.mean(values, axis=-1, keepdims=True)
    inverse = lax.rsqrt(jnp.mean(center * center, axis=-1, keepdims=True) + NORM_EPS)
    return center * inverse, inverse


def norm_back(grad_in, normed, inverse, gain):
    scaled = grad_in * gain
    return inverse * (
        scaled
        - jnp.mean(scaled, axis=-1, keepdims=True)
        - normed * jnp.mean(scaled * normed, axis=-1, keepdims=True)
    )


def colsum(v):
    return jnp.sum(v, axis=0, keepdims=True)


def assemble(scratch, half_ref, relayed_ref, side):
    rows = half_ref.shape[0]
    here, there = half_ref[...], relayed_ref[...]
    scratch[0:rows, :] = jnp.where(side == 0, here, there)
    scratch[rows : 2 * rows, :] = jnp.where(side == 0, there, here)


def prepare(where_ref, qkv_ref, out_ref, perm_ref, vec_ref, packed_ref, half_ref, small_ref, lines_ref):
    width = qkv_ref.shape[1]
    turned = out_ref[...].astype(F32).T.astype(BF16)
    heads = qkv_ref.shape[2] // HEAD_DIM
    for h in range(heads):
        cut = slice(h * HEAD_DIM, (h + 1) * HEAD_DIM)
        packed_ref[:, h * SLOT : (h + 1) * SLOT] = jnp.concatenate(
            [qkv_ref[0, :, cut], qkv_ref[2, :, cut], qkv_ref[1, :, cut], turned[:, cut]], axis=1
        )
    half = width // 2
    half_ref[...] = jnp.where(where_ref[0] == 0, packed_ref[0:half, :], packed_ref[half:width, :])
    lines = vec_ref[...].astype(F32)
    lines_ref[...] = lines
    seqs = perm_ref.shape[0]
    for s in range(seqs):
        small_ref[s * heads : (s + 1) * heads, :] = perm_ref[s].astype(F32)
    own = heads * HEAD_DIM
    blank = jnp.zeros((1, 2 * HEAD_DIM), F32)
    bias = []
    for h in range(heads):
        bias += [lines[7:8, h * HEAD_DIM : (h + 1) * HEAD_DIM], lines[7:8, own + h * HEAD_DIM : own + (h + 1) * HEAD_DIM], blank]
    length = small_ref.shape[1]
    for row, line in ((seqs * heads, lines[6:7, :]), (seqs * heads + 2, jnp.concatenate(bias, axis=1))):
        small_ref[row : row + 1, :] = line[:, 0:length]
        rest = line.shape[1] - length
        small_ref[row + 1 : row + 2, :] = jnp.concatenate([line[:, length:], jnp.zeros((1, length - rest), F32)], axis=1)


def unpack(packed_ref, qkv_ref, out_ref, vec_ref):
    width = packed_ref.shape[1]
    heads = width // SLOT
    rows = qkv_ref.shape[1]

    def field(at):
        return jnp.concatenate(
            [packed_ref[0:rows, h * SLOT + at * HEAD_DIM : h * SLOT + (at + 1) * HEAD_DIM] for h in range(heads)], axis=1
        ).astype(F32)

    qkv_ref[0], qkv_ref[2], qkv_ref[1] = field(0), field(1), field(2)
    out_ref[...] = field(3).T
    vec_ref[...] = packed_ref[rows : rows + 16, :].astype(F32)


def put_orders(where_ref, packs, seg_ref, order_ref, turned_ref):
    heads = order_ref.shape[0] // 2 - 1
    order_ref[...] = jnp.zeros_like(order_ref)
    for group, pack in enumerate(packs):
        for h in range(heads):
            at = group * heads + h
            order_ref[at : at + 1, :] = pack[pl.ds(where_ref[1] * heads + h, 1), :]
    order_ref[2 * heads : 2 * heads + 1, :] = seg_ref[pl.ds(where_ref[1], 1), :].astype(F32)
    turned_ref[...] = order_ref[...].T


def put_tables(order_ref, turned_ref, count, place_ref, position_ref):
    length = order_ref.shape[1]
    lane = lax.broadcasted_iota(jnp.int32, (length, length), 1).astype(F32)
    sub = lax.broadcasted_iota(jnp.int32, (length, length), 0).astype(F32)
    for at in range(count):
        place_ref[at] = jnp.where(turned_ref[:, at : at + 1] == lane, 1.0, 0.0).astype(BF16)
        position_ref[at] = jnp.where(order_ref[at : at + 1, :] == sub, 1.0, 0.0).astype(BF16)


def put_out_columns(weights, columns_ref):
    heads = weights[0].shape[1] // SLOT
    for group, w_ref in enumerate(weights):
        for h in range(heads):
            at = group * heads + h
            columns_ref[:, at * PAIR : (at + 1) * PAIR] = w_ref[:, h * SLOT + PAIR : (h + 1) * SLOT]


def cuts(length):
    return [slice(c, c + CLUSTER) for c in range(0, length, CLUSTER)]


def attend(
    x_ref, weights, packs, order_ref, turned_ref, fields_ref, probs_ref, ctx_ref,
    place_ref, position_ref, raw_ref, scores_ref, columns_ref,
):
    length = x_ref.shape[0]
    heads = weights[0].shape[1] // SLOT
    count = 2 * heads
    lanes = lax.broadcasted_iota(jnp.int32, (length, SLOT), 1)
    bias_row = packs[0].shape[0] - 2
    for group, (w_ref, pack) in enumerate(zip(weights, packs)):
        bias = jnp.concatenate([pack[bias_row : bias_row + 1, :], pack[bias_row + 1 : bias_row + 2, :]], axis=1)
        for h in range(heads):
            fields = mm(x_ref[...], w_ref[:, h * SLOT : (h + 1) * SLOT]) + bias[:, h * SLOT : (h + 1) * SLOT]
            raw_ref[group * heads + h] = jnp.where(lanes < 3 * HEAD_DIM, fields, turned_ref[:, count : count + 1]).astype(BF16)
    put_tables(order_ref, turned_ref, count, place_ref, position_ref)
    order_low = order_ref[...].astype(BF16)
    seg_rows = []
    for at in range(count):
        fields_ref[at] = mm(place_ref[at], raw_ref[at]).astype(BF16)
        seg_rows.append(mm(order_low, position_ref[at])[count : count + 1, :])
    for at in range(count):
        for c, cut in enumerate(cuts(length)):
            seg_col = fields_ref[at, cut, SLOT - PAIR : SLOT].astype(F32)[:, PAIR - 1 : PAIR]
            scores = mm_nt(fields_ref[at, cut, 0:HEAD_DIM], fields_ref[at, cut, PAIR : PAIR + HEAD_DIM]) * SCALE
            scores_ref[at, cut, :] = jnp.where(seg_col == seg_rows[at][:, cut], scores, MASKED)
    for at in range(count):
        for cut in cuts(length):
            scores = scores_ref[at, cut, :]
            raised = jnp.exp(scores - jnp.max(scores, axis=-1, keepdims=True))
            probs_ref[at, cut, :] = (raised / jnp.sum(raised, axis=-1, keepdims=True)).astype(BF16)
    low_lanes = lax.broadcasted_iota(jnp.int32, (CLUSTER, PAIR), 1) < HEAD_DIM
    for at in range(count):
        for cut in cuts(length):
            mixed = mm(probs_ref[at, cut, :], fields_ref[at, cut, 0:PAIR])
            raw_ref[at, cut, 0:PAIR] = jnp.where(low_lanes, 0.0, mixed).astype(BF16)
    for at in range(count):
        ctx_ref[:, at * PAIR : (at + 1) * PAIR] = mm(position_ref[at], raw_ref[at, :, 0:PAIR]).astype(BF16)
    put_out_columns(weights, columns_ref)


def near_attention(
    where_ref, x_ref, w0_ref, w1_ref, pack0_ref, pack1_ref, seg_ref,
    fields_ref, probs_ref, ctx_ref, sum_ref, order_ref, turned_ref,
    place_ref, position_ref, raw_ref, scores_ref, columns_ref,
):
    packs = (pack0_ref, pack1_ref)
    put_orders(where_ref, packs, seg_ref, order_ref, turned_ref)
    attend(
        x_ref, (w0_ref, w1_ref), packs, order_ref, turned_ref, fields_ref, probs_ref, ctx_ref,
        place_ref, position_ref, raw_ref, scores_ref, columns_ref,
    )
    sum_ref[...] = mm_nt(ctx_ref[...], columns_ref[...])


def blocks(length):
    return [slice(r, r + BLOCK) for r in range(0, length, BLOCK)]


def far_attention(
    where_ref, x_ref, a2_ref, b2_ref, a3_ref, b3_ref, pack2_ref, pack3_ref, seg_ref, sum_ref, vec_ref,
    fields_ref, probs_ref, ctx_ref, order_ref, turned_ref, low_ref, normed_ref, inverse_ref,
    place_ref, position_ref, raw_ref, scores_ref, columns_ref, w2_ref, w3_ref, total_ref,
):
    packs = (pack2_ref, pack3_ref)
    assemble(w2_ref, a2_ref, b2_ref, where_ref[0])
    assemble(w3_ref, a3_ref, b3_ref, where_ref[0])
    put_orders(where_ref, packs, seg_ref, order_ref, turned_ref)
    attend(
        x_ref, (w2_ref, w3_ref), packs, order_ref, turned_ref, fields_ref, probs_ref, ctx_ref,
        place_ref, position_ref, raw_ref, scores_ref, columns_ref,
    )
    total_ref[...] = mm_nt(ctx_ref[...], columns_ref[...])
    for r in blocks(x_ref.shape[0]):
        normed, inverse = norm(x_ref[r, :].astype(F32) + sum_ref[r, :] + total_ref[r, :] + vec_ref[0:1, :])
        low_ref[r, :] = (normed * vec_ref[1:2, :] + vec_ref[2:3, :]).astype(BF16)
        normed_ref[r, :] = normed
        inverse_ref[r, :] = inverse


def up_bias(pack_ref, width):
    row = pack_ref.shape[0] - 4
    return jnp.concatenate([pack_ref[row : row + 1, :], pack_ref[row + 1 : row + 2, :]], axis=1)[:, 0:width]


def hidden_units(low_ref, up_ref, shift, hidden_ref, slope_ref):
    length = low_ref.shape[0]
    for r in blocks(length):
        v = mm(low_ref[r, :], up_ref[...]) + shift
        half = 0.5 + 0.5 * lax.erf(v * ROOT_HALF)
        hidden_ref[r, :] = (v * half).astype(BF16)
        slope_ref[r, :] = (half + v * jnp.exp(-0.5 * v * v) * INV_ROOT_TWO_PI).astype(BF16)


def near_forward(low_ref, u0_ref, u1_ref, d0_ref, d1_ref, pack0_ref, pack1_ref, hidden_ref, slope_ref, sum_ref):
    width = u0_ref.shape[1]
    hidden_units(low_ref, u0_ref, up_bias(pack0_ref, width), hidden_ref.at[0], slope_ref.at[0])
    hidden_units(low_ref, u1_ref, up_bias(pack1_ref, width), hidden_ref.at[1], slope_ref.at[1])
    for r in blocks(low_ref.shape[0]):
        sum_ref[r, :] = mm(hidden_ref[0, r, :], d0_ref[...]) + mm(hidden_ref[1, r, :], d1_ref[...])


def far_up(where_ref, low_ref, a2_ref, b2_ref, a3_ref, b3_ref, pack2_ref, pack3_ref, hidden_ref, slope_ref, u2_ref, u3_ref):
    width = a2_ref.shape[1]
    assemble(u2_ref, a2_ref, b2_ref, where_ref[0])
    assemble(u3_ref, a3_ref, b3_ref, where_ref[0])
    hidden_units(low_ref, u2_ref, up_bias(pack2_ref, width), hidden_ref.at[0], slope_ref.at[0])
    hidden_units(low_ref, u3_ref, up_bias(pack3_ref, width), hidden_ref.at[1], slope_ref.at[1])


def far_down(
    where_ref, hidden_ref, a2_ref, b2_ref, a3_ref, b3_ref, sum_ref, normed_a_ref, cot_ref, vec_ref,
    out_ref, grad_ref, grad_low_ref, sums_ref, d2_ref, d3_ref,
):
    assemble(d2_ref, a2_ref, b2_ref, where_ref[0])
    assemble(d3_ref, a3_ref, b3_ref, where_ref[0])
    sums_ref[...] = jnp.zeros_like(sums_ref)
    for r in blocks(hidden_ref.shape[1]):
        total = sum_ref[r, :] + mm(hidden_ref[0, r, :], d2_ref[...]) + mm(hidden_ref[1, r, :], d3_ref[...])
        middle = normed_a_ref[r, :] * vec_ref[1:2, :] + vec_ref[2:3, :]
        normed, inverse = norm(middle + total + vec_ref[3:4, :])
        out_ref[r, :] = (normed * vec_ref[4:5, :] + vec_ref[5:6, :]).astype(BF16)
        cot = cot_ref[r, :].astype(F32)
        grad = norm_back(cot, normed, inverse, vec_ref[4:5, :])
        grad_ref[r, :] = grad
        grad_low_ref[r, :] = grad.astype(BF16)
        sums_ref[0:1, :] += colsum(cot * normed)
        sums_ref[1:2, :] += colsum(cot)
        sums_ref[2:3, :] += colsum(grad)


def down_grads(far_ref, near_ref, grad_low_ref, g3_ref, g2_ref, g1_ref, g0_ref):
    g3_ref[...] = mm_tn(far_ref[1], grad_low_ref[...]).astype(BF16)
    g2_ref[...] = mm_tn(far_ref[0], grad_low_ref[...]).astype(BF16)
    g1_ref[...] = mm_tn(near_ref[1], grad_low_ref[...]).astype(BF16)
    g0_ref[...] = mm_tn(near_ref[0], grad_low_ref[...]).astype(BF16)


def up_grads(grad_low_ref, low_ref, slope_ref, down_ref, up_ref, pre_ref, out_ref, mid_ref, first, sums_ref, at):
    pre = (mm_nt(grad_low_ref[...], down_ref[...]) * slope_ref[...].astype(F32)).astype(BF16)
    pre_ref[...] = pre
    sums_ref[at : at + 1, :] = colsum(pre.astype(F32))
    out_ref[...] = mm_tn(low_ref[...], pre_ref[...]).astype(BF16)
    part = mm_nt(pre_ref[...], up_ref[...])
    mid_ref[...] = part if first else mid_ref[...] + part


def far_up_grads(
    where_ref, grad_low_ref, low_ref, slope_ref, d2a_ref, d2b_ref, d3a_ref, d3b_ref, u2a_ref, u2b_ref, u3a_ref, u3b_ref,
    g3_ref, g2_ref, mid_ref, shift_ref, d2_ref, d3_ref, u2_ref, u3_ref, pre2_ref, pre3_ref,
):
    side = where_ref[0]
    shift_ref[...] = jnp.zeros_like(shift_ref)
    assemble(d3_ref, d3a_ref, d3b_ref, side)
    assemble(u3_ref, u3a_ref, u3b_ref, side)
    assemble(d2_ref, d2a_ref, d2b_ref, side)
    assemble(u2_ref, u2a_ref, u2b_ref, side)
    up_grads(grad_low_ref, low_ref, slope_ref.at[1], d3_ref, u3_ref, pre3_ref, g3_ref, mid_ref, True, shift_ref, 1)
    up_grads(grad_low_ref, low_ref, slope_ref.at[0], d2_ref, u2_ref, pre2_ref, g2_ref, mid_ref, False, shift_ref, 0)


def near_up_grads(
    grad_low_ref, low_ref, slope_ref, d0_ref, d1_ref, u0_ref, u1_ref, far_mid_ref, grad_b_ref, normed_ref, inverse_ref,
    vec_ref, g1_ref, g0_ref, grad_ref, grad_out_ref, shift_ref, sums_ref, pre0_ref, pre1_ref, mid_ref,
):
    shift_ref[...] = jnp.zeros_like(shift_ref)
    sums_ref[...] = jnp.zeros_like(sums_ref)
    up_grads(grad_low_ref, low_ref, slope_ref.at[1], d1_ref, u1_ref, pre1_ref, g1_ref, mid_ref, True, shift_ref, 1)
    up_grads(grad_low_ref, low_ref, slope_ref.at[0], d0_ref, u0_ref, pre0_ref, g0_ref, mid_ref, False, shift_ref, 0)
    for r in blocks(low_ref.shape[0]):
        total = mid_ref[r, :] + far_mid_ref[r, :] + grad_b_ref[r, :]
        normed = normed_ref[r, :]
        grad = norm_back(total, normed, inverse_ref[r, :], vec_ref[1:2, :])
        grad_ref[r, :] = grad
        grad_out_ref[r, :] = grad.astype(BF16)
        sums_ref[0:1, :] += colsum(total * normed)
        sums_ref[1:2, :] += colsum(total)
        sums_ref[2:3, :] += colsum(grad)


def attend_back(
    x_ref, grad_out_ref, weights, order_ref, turned_ref, fields_ref, probs_ref, ctx_ref, outs,
    sums_b_ref, sums_a_ref, shift_ref, place_ref, position_ref, columns_ref, grads_ref, moved_ref, raw_ref, tok_ref, scores_ref, low_ref,
):
    length, width = x_ref.shape
    heads = weights[0].shape[1] // SLOT
    count = 2 * heads
    put_tables(order_ref, turned_ref, count, place_ref, position_ref)
    put_out_columns(weights, columns_ref)
    grads_ref[...] = mm(grad_out_ref[...], columns_ref[...]).astype(BF16)
    for at in range(count):
        moved_ref[at] = mm(place_ref[at], grads_ref[:, at * PAIR : (at + 1) * PAIR]).astype(BF16)
    low_lanes = lax.broadcasted_iota(jnp.int32, (CLUSTER, PAIR), 1) < HEAD_DIM
    no_low = jnp.zeros((CLUSTER, PAIR), BF16)
    for at in range(count):
        for cut in cuts(length):
            values = jnp.where(low_lanes, no_low, fields_ref[at, cut, 0:PAIR])
            scores_ref[at, cut, :] = mm_nt(moved_ref[at, cut, :], values)
    for at in range(count):
        for cut in cuts(length):
            grad_probs = scores_ref[at, cut, :]
            probs = probs_ref[at, cut, :].astype(F32)
            delta = jnp.sum(grad_probs * probs, axis=-1, keepdims=True)
            low_ref[at, cut, :] = (probs * (grad_probs - delta)).astype(BF16)
    for at in range(count):
        for cut in cuts(length):
            grad_queries = mm(low_ref[at, cut, :], fields_ref[at, cut, PAIR:SLOT]) * SCALE
            grad_values = mm_tn(probs_ref[at, cut, :], moved_ref[at, cut, :])
            raw_ref[at, cut, 0:PAIR] = jnp.where(low_lanes, grad_queries, grad_values).astype(BF16)
    for at in range(count):
        for cut in cuts(length):
            grad_keys = mm_tn(low_ref[at, cut, :], fields_ref[at, cut, 0:PAIR]) * SCALE
            raw_ref[at, cut, PAIR:SLOT] = jnp.where(low_lanes, grad_keys, 0.0).astype(BF16)
    for group, out_ref in reversed(list(enumerate(outs))):
        for h in range(heads):
            at = group * heads + h
            tok_ref[group, :, h * SLOT : (h + 1) * SLOT] = mm(position_ref[at], raw_ref[at]).astype(BF16)
        out_grad = mm_tn(grad_out_ref[...], ctx_ref[:, group * heads * PAIR : (group + 1) * heads * PAIR])
        grad = mm_tn(x_ref[...], tok_ref[group])
        for h in range(heads):
            out_ref[0:width, h * SLOT : h * SLOT + PAIR] = grad[:, h * SLOT : h * SLOT + PAIR].astype(BF16)
            out_ref[0:width, h * SLOT + PAIR : (h + 1) * SLOT] = (
                grad[:, h * SLOT + PAIR : (h + 1) * SLOT] + out_grad[:, h * PAIR : (h + 1) * PAIR]
            ).astype(BF16)
        fields = colsum(tok_ref[group].astype(F32))
        block = jnp.concatenate([sums_b_ref[0:3, :], sums_a_ref[0:3, :], shift_ref[group : group + 1, :], fields], axis=0)
        zero = jnp.zeros((EXTRA - 8, width), F32)
        out_ref[width:, :] = jnp.concatenate([block, zero], axis=0).astype(BF16)


def far_attention_grads(
    where_ref, x_ref, grad_out_ref, a2_ref, b2_ref, a3_ref, b3_ref, order_ref, turned_ref, fields_ref, probs_ref, ctx_ref,
    sums_b_ref, sums_a_ref, shift_ref, g3_ref, g2_ref, sum_ref,
    place_ref, position_ref, columns_ref, grads_ref, moved_ref, raw_ref, tok_ref, scores_ref, low_ref, w2_ref, w3_ref,
):
    assemble(w2_ref, a2_ref, b2_ref, where_ref[0])
    assemble(w3_ref, a3_ref, b3_ref, where_ref[0])
    attend_back(
        x_ref, grad_out_ref, (w2_ref, w3_ref), order_ref, turned_ref, fields_ref, probs_ref, ctx_ref, (g2_ref, g3_ref),
        sums_b_ref, sums_a_ref, shift_ref, place_ref, position_ref, columns_ref, grads_ref, moved_ref, raw_ref, tok_ref, scores_ref, low_ref,
    )
    sum_ref[...] = mm_nt(tok_ref[0], w2_ref[...]) + mm_nt(tok_ref[1], w3_ref[...])


def near_attention_grads(
    x_ref, grad_out_ref, w0_ref, w1_ref, order_ref, turned_ref, fields_ref, probs_ref, ctx_ref,
    sums_b_ref, sums_a_ref, shift_ref, sum_ref, grad_a_ref, g1_ref, g0_ref, in_ref,
    place_ref, position_ref, columns_ref, grads_ref, moved_ref, raw_ref, tok_ref, scores_ref, low_ref,
):
    attend_back(
        x_ref, grad_out_ref, (w0_ref, w1_ref), order_ref, turned_ref, fields_ref, probs_ref, ctx_ref, (g0_ref, g1_ref),
        sums_b_ref, sums_a_ref, shift_ref, place_ref, position_ref, columns_ref, grads_ref, moved_ref, raw_ref, tok_ref, scores_ref, low_ref,
    )
    in_ref[...] = (mm_nt(tok_ref[0], w0_ref[...]) + mm_nt(tok_ref[1], w1_ref[...]) + sum_ref[...] + grad_a_ref[...]).astype(BF16)


def solution(mesh):
    dp_size, tensor_size = mesh.shape["dp"], mesh.shape["tensor"]
    levels = dp_size.bit_length() - 1

    def swap(v, axis, bit):
        size = tensor_size if axis == "tensor" else dp_size
        return lax.ppermute(v, axis, [(i, i ^ (1 << bit)) for i in range(size)])

    def core_swap(v):
        return swap(v, "tensor", 0)

    def chip_swap(v):
        return swap(v, "tensor", 1)

    def add(a, b):
        return lax.reduce_precision(a.astype(F32) + b.astype(F32), 8, 7).astype(BF16)

    def on_device(
        layer_input, out_cotangent, qkv_weight, qv_bias, out_weight, out_bias, norm1_gain, norm1_bias,
        up_weight, up_bias, down_weight, down_bias, norm2_gain, norm2_bias, cluster_perm, segment_ids,
    ):
        length, width = layer_input.shape
        seqs, heads, _ = cluster_perm.shape
        units = up_weight.shape[1]
        mine = lax.axis_index("tensor")
        place = lax.axis_index("dp")
        side = place & 1
        half = width // 2

        where_arg = jnp.stack([side, mine]).astype(jnp.int32)
        count = 2 * heads
        lines = jnp.concatenate(
            [out_bias, norm1_gain, norm1_bias, down_bias, norm2_gain, norm2_bias, up_bias, qv_bias.reshape(-1),
             jnp.zeros((2 * width - units - 2 * heads * HEAD_DIM,), BF16)]
        ).reshape(8, width)
        square, half_t = ((width, width), BF16), ((half, width), BF16)
        vec_t = ((8, width), F32)
        small_t = ((seqs * heads + 4, length), F32)
        packed, packed_half, small, vecs = call(
            prepare, [square, half_t, small_t, vec_t], [], 3, where_arg, qkv_weight, out_weight, cluster_perm, lines
        )

        def own_half(m):
            return lax.dynamic_slice_in_dim(m, side * half, half, axis=0)

        def gather(m, m_half):
            first = chip_swap(m_half)
            second = swap(first, "dp", 0)
            return core_swap(m), (first, second, core_swap(first), core_swap(second))

        small_2, small_1 = chip_swap(small), core_swap(small)
        halves = [packed_half, own_half(up_weight), own_half(down_weight)]
        c_first, u_first, d_first = [chip_swap(m) for m in halves]
        c1, u1, d1 = core_swap(packed), core_swap(up_weight), core_swap(down_weight)

        def relay(first):
            second = swap(first, "dp", 0)
            return first, second, core_swap(first), second

        fields_t = ((count, length, SLOT), BF16)
        probs_t = ((count, length, CLUSTER), BF16)
        ctx_t = ((length, count * PAIR), BF16)
        orders_t = [((8, length), F32), ((length, 8), F32)]
        rows_f, rows_b = ((length, width), F32), ((length, width), BF16)
        pair_b = ((2, length, units), BF16)
        tall = ((width + EXTRA, heads * SLOT), BF16)
        mat, rows_s = pltpu.VMEM((width, width), BF16), pltpu.VMEM((length, width), BF16)
        tables = [pltpu.VMEM((count, length, length), BF16)] * 2
        columns = pltpu.VMEM((width, count * PAIR), BF16)
        raw = pltpu.VMEM((count, length, SLOT), BF16)
        scores = pltpu.VMEM((count, length, CLUSTER), F32)
        back = tables + [columns, rows_s, pltpu.VMEM((count, length, PAIR), BF16), raw, pltpu.VMEM((2, length, width), BF16)]
        back += [scores, pltpu.VMEM((count, length, CLUSTER), BF16)]

        near_fields, near_probs, near_ctx, attn_sum, *near_orders = call(
            near_attention, [fields_t, probs_t, ctx_t, rows_f, *orders_t], [*tables, raw, scores, columns], 8,
            where_arg, layer_input, packed, c1, small, small_1, segment_ids, after=(small_2,),
        )
        small_3 = core_swap(small_2)
        c_far = relay(tie(c_first, attn_sum))
        c_far = (*c_far[:3], core_swap(c_far[3]))
        u_far = relay(tie(u_first, attn_sum))
        far_fields, far_probs, far_ctx, *far_orders, low, normed_a, inverse_a = call(
            far_attention, [fields_t, probs_t, ctx_t, *orders_t, rows_b, rows_f, ((length, 1), F32)],
            [*tables, raw, scores, columns, mat, mat, pltpu.VMEM((length, width), F32)], 1,
            where_arg, layer_input, *c_far, small_2, small_3, segment_ids, attn_sum, vecs,
        )
        u_far = (*u_far[:3], core_swap(tie(u_far[3], low)))
        d_far = relay(tie(d_first, low))
        near_hidden, near_slope, ffn_sum = call(
            near_forward, [pair_b, pair_b, rows_f], [], 6, low, up_weight, u1, down_weight, d1, small, small_1
        )
        far_hidden, far_slope = call(
            far_up, [pair_b, pair_b], [mat, mat], 5, where_arg, low, *u_far, small_2, small_3
        )
        d_far = (*d_far[:3], core_swap(tie(d_far[3], ffn_sum, far_hidden)))
        layer_output, grad_b, grad_b_low, sums_b = call(
            far_down, [rows_b, rows_f, rows_b, vec_t], [mat, mat], 5,
            where_arg, far_hidden, *d_far, ffn_sum, normed_a, out_cotangent, vecs,
        )
        dg3, dg2, dg1, dg0 = call(down_grads, [square] * 4, [], 2.8, far_hidden, near_hidden, grad_b_low)
        ds3, ds1 = core_swap(dg3), core_swap(dg1)
        ug3, ug2, grad_mid, far_ub = call(
            far_up_grads, [square, square, rows_f, vec_t], [mat] * 4 + [rows_s] * 2, 0.1,
            where_arg, grad_b_low, low, far_slope, *d_far, *u_far,
        )
        us3 = core_swap(ug3)
        down_cross = add(dg2, tie(ds3, grad_mid))
        ug1, ug0, grad_a, grad_a_low, near_ub, sums_a = call(
            near_up_grads, [square, square, rows_f, rows_b, vec_t, vec_t], [rows_s, rows_s, pltpu.VMEM((length, width), F32)], 0.1,
            grad_b_low, low, near_slope, down_weight, d1, up_weight, u1, grad_mid, grad_b, normed_a, inverse_a, vecs,
            after=(down_cross,),
        )
        us1 = core_swap(ug1)
        up_cross = add(ug2, tie(us3, grad_a_low))
        cg3, cg2, in_sum = call(
            far_attention_grads, [tall, tall, rows_f], back + [mat, mat], 0.1,
            where_arg, layer_input, grad_a_low, *c_far, *far_orders, far_fields, far_probs, far_ctx, sums_b, sums_a, far_ub,
            after=(up_cross,),
        )
        cs3 = core_swap(cg3)
        down_total = add(add(dg0, ds1), tie(chip_swap(down_cross), in_sum))
        packed_cross = add(cg2, cs3)
        cg1, cg0, input_grad = call(
            near_attention_grads, [tall, tall, rows_b], back, 0.1,
            layer_input, grad_a_low, packed, c1, *near_orders, near_fields, near_probs, near_ctx,
            sums_b, sums_a, near_ub, in_sum, grad_a, after=(down_total, packed_cross),
        )
        steps = [(level, True) for level in range(levels)] + [(level, False) for level in reversed(range(levels))]

        def step(total, at, *others):
            level, halve = steps[at]
            bit = (place >> level) & 1
            if halve:
                rows = total.shape[0] // 2
                send = lax.dynamic_slice_in_dim(total, (1 - bit) * rows, rows, axis=0)
                keep = lax.dynamic_slice_in_dim(total, bit * rows, rows, axis=0)
                return add(keep, tie(swap(send, "dp", level), *others))
            other = tie(swap(total, "dp", level), *others)
            return jnp.where(
                bit == 0, jnp.concatenate([total, other], axis=0), jnp.concatenate([other, total], axis=0)
            )

        last = len(steps) - 1
        down, up, whole = [down_total], [], []

        def reach(chain, at, *others):
            while len(chain) < min(at, last) + 2:
                chain.append(step(chain[-1], len(chain) - 1, *others))
            return chain[-1]

        reach(down, 0, input_grad)
        up.append(add(add(ug0, us1), tie(chip_swap(up_cross), down[-1])))
        reach(down, 2)
        reach(up, 0)
        whole.append(add(add(cg0, core_swap(cg1)), tie(chip_swap(packed_cross), down[-1], up[-1])))
        for at in range(last + 1):
            reach(down, at + 4)
            reach(up, at + 2)
            reach(whole, at, down[-1], up[-1])
        down_grad, up_grad, packed_grad = down[-1].astype(F32), up[-1].astype(F32), whole[-1]
        qkv_grad, out_grad, sums = call(
            unpack,
            [((3, width, heads * HEAD_DIM), F32), ((heads * HEAD_DIM, width), F32), ((16, width), F32)], [], 1,
            packed_grad,
        )
        field_sums = sums[7].reshape(heads, 4, HEAD_DIM)
        qv_grad = jnp.stack([field_sums[:, 0].reshape(-1), field_sums[:, 1].reshape(-1)])
        return (
            layer_output, input_grad, qkv_grad, qv_grad, out_grad, sums[5], sums[3], sums[4],
            up_grad, sums[6], down_grad, sums[2], sums[0], sums[1],
        )

    rows, split, copied = P(("dp", "tensor"), None), P(None, "tensor"), P()
    in_specs = (
        rows, rows, P(None, None, "tensor"), split, P("tensor", None), copied, copied, copied, split, P("tensor"),
        P("tensor", None), copied, copied, copied, P("dp", "tensor", None), P("dp", None),
    )
    out_specs = (
        rows, rows, P(None, None, "tensor"), split, P("tensor", None), copied, copied, copied, split, P("tensor"),
        P("tensor", None), copied, copied, copied,
    )
    return jax.shard_map(on_device, mesh=mesh, in_specs=in_specs, out_specs=out_specs, check_vma=False)
```

```python
import math

import jax
import jax.numpy as jnp
from jax import lax
from jax.experimental import pallas as pl
from jax.experimental.pallas import tpu as pltpu
from jax.sharding import PartitionSpec as P

HEAD_DIM = 64
CLUSTER = 128
NORM_EPS = 1e-12
MASKED = -1000000000.0
ROOT_HALF = 0.7071067811865476
INV_ROOT_TWO_PI = 0.3989422804014327
SCALE = 1.0 / math.sqrt(HEAD_DIM)
SLOT = 4 * HEAD_DIM
PAIR = 2 * HEAD_DIM
BLOCK = 128
VMEM_LIMIT = 30 * 1024 * 1024
EXTRA = 64
F32 = jnp.float32
BF16 = jnp.bfloat16


def mm(a, b):
    return jnp.dot(a, b, preferred_element_type=F32)


def mm_nt(a, b):
    return lax.dot_general(a, b, (((1,), (1,)), ((), ())), preferred_element_type=F32)


def mm_tn(a, b):
    return lax.dot_general(a, b, (((0,), (0,)), ((), ())), preferred_element_type=F32)


def call(body, outs, scratch, micros, *args, after=(), apart=0):
    shapes = [jax.ShapeDtypeStruct(s, t) for s, t in outs]
    kept = len(args)

    def placed(a):
        flat = a.ndim == 1 and a.dtype == jnp.int32
        return pl.BlockSpec(memory_space=pltpu.SMEM if flat else pltpu.VMEM)

    def run(*refs):
        body(*refs[:kept], *refs[kept + len(after) :])

    return pl.pallas_call(
        run,
        out_shape=shapes,
        in_specs=[placed(a) for a in args] + [pl.BlockSpec(memory_space=pl.ANY)] * len(after),
        out_specs=[pl.BlockSpec(memory_space=pltpu.HBM if i < apart else pltpu.VMEM) for i in range(len(outs))],
        scratch_shapes=scratch,
        cost_estimate=pl.CostEstimate(flops=int(micros * 1e9), bytes_accessed=0, transcendentals=0),
        compiler_params=pltpu.CompilerParams(vmem_limit_bytes=VMEM_LIMIT),
    )(*args, *after)


def tie(value, *others):
    return lax.optimization_barrier((value, *others))[0]


def norm(values):
    center = values - jnp.mean(values, axis=-1, keepdims=True)
    inverse = lax.rsqrt(jnp.mean(center * center, axis=-1, keepdims=True) + NORM_EPS)
    return center * inverse, inverse


def norm_back(grad_in, normed, inverse, gain):
    scaled = grad_in * gain
    return inverse * (
        scaled
        - jnp.mean(scaled, axis=-1, keepdims=True)
        - normed * jnp.mean(scaled * normed, axis=-1, keepdims=True)
    )


def colsum(v):
    return jnp.sum(v, axis=0, keepdims=True)


def assemble(scratch, half_ref, relayed_ref, side):
    rows = half_ref.shape[0]
    here, there = half_ref[...], relayed_ref[...]
    scratch[0:rows, :] = jnp.where(side == 0, here, there)
    scratch[rows : 2 * rows, :] = jnp.where(side == 0, there, here)


def prepare(where_ref, qkv_ref, out_ref, perm_ref, vec_ref, packed_ref, half_ref, small_ref, lines_ref):
    width = qkv_ref.shape[1]
    turned = out_ref[...].astype(F32).T.astype(BF16)
    heads = qkv_ref.shape[2] // HEAD_DIM
    for h in range(heads):
        cut = slice(h * HEAD_DIM, (h + 1) * HEAD_DIM)
        packed_ref[:, h * SLOT : (h + 1) * SLOT] = jnp.concatenate(
            [qkv_ref[0, :, cut], qkv_ref[2, :, cut], qkv_ref[1, :, cut], turned[:, cut]], axis=1
        )
    half = width // 2
    half_ref[...] = jnp.where(where_ref[0] == 0, packed_ref[0:half, :], packed_ref[half:width, :])
    lines = vec_ref[...].astype(F32)
    lines_ref[...] = lines
    seqs = perm_ref.shape[0]
    for s in range(seqs):
        small_ref[s * heads : (s + 1) * heads, :] = perm_ref[s].astype(F32)
    own = heads * HEAD_DIM
    blank = jnp.zeros((1, 2 * HEAD_DIM), F32)
    bias = []
    for h in range(heads):
        bias += [lines[7:8, h * HEAD_DIM : (h + 1) * HEAD_DIM], lines[7:8, own + h * HEAD_DIM : own + (h + 1) * HEAD_DIM], blank]
    length = small_ref.shape[1]
    for row, line in ((seqs * heads, lines[6:7, :]), (seqs * heads + 2, jnp.concatenate(bias, axis=1))):
        small_ref[row : row + 1, :] = line[:, 0:length]
        rest = line.shape[1] - length
        small_ref[row + 1 : row + 2, :] = jnp.concatenate([line[:, length:], jnp.zeros((1, length - rest), F32)], axis=1)


def unpack(packed_ref, qkv_out_ref, out_ref, vec_ref, bias_ref, qkv_ref, sems):
    width = packed_ref.shape[1]
    heads = width // SLOT
    rows = qkv_ref.shape[2]

    def field(at):
        return jnp.concatenate(
            [packed_ref[0:rows, h * SLOT + at * HEAD_DIM : h * SLOT + (at + 1) * HEAD_DIM] for h in range(heads)], axis=1
        ).astype(F32)

    copies = []
    for at, member in enumerate((0, 2, 1)):
        qkv_ref[member] = field(at).T
        copies.append(pltpu.make_async_copy(qkv_ref.at[member], qkv_out_ref.at[member], sems.at[at]))
        copies[-1].start()
    out_ref[...] = field(3).T
    vectors = packed_ref[rows : rows + 16, :].astype(F32)
    vec_ref[...] = vectors
    for member in range(2):
        starts = [h * SLOT + member * HEAD_DIM for h in range(heads)]
        bias_ref[member : member + 1, :] = jnp.concatenate([vectors[7:8, c : c + HEAD_DIM] for c in starts], axis=1)
    for copy in copies:
        copy.wait()


def put_orders(where_ref, packs, seg_ref, order_ref, turned_ref):
    heads = order_ref.shape[0] // 2 - 1
    order_ref[...] = jnp.zeros_like(order_ref)
    for group, pack in enumerate(packs):
        for h in range(heads):
            at = group * heads + h
            order_ref[at : at + 1, :] = pack[pl.ds(where_ref[1] * heads + h, 1), :]
    order_ref[2 * heads : 2 * heads + 1, :] = seg_ref[pl.ds(where_ref[1], 1), :].astype(F32)
    turned_ref[...] = order_ref[...].T


def put_tables(order_ref, turned_ref, count, place_ref, position_ref):
    length = order_ref.shape[1]
    lane = lax.broadcasted_iota(jnp.int32, (length, length), 1).astype(F32)
    sub = lax.broadcasted_iota(jnp.int32, (length, length), 0).astype(F32)
    for at in range(count):
        place_ref[at] = jnp.where(turned_ref[:, at : at + 1] == lane, 1.0, 0.0).astype(BF16)
        position_ref[at] = jnp.where(order_ref[at : at + 1, :] == sub, 1.0, 0.0).astype(BF16)


def put_out_columns(weights, columns_ref):
    heads = weights[0].shape[1] // SLOT
    for group, w_ref in enumerate(weights):
        for h in range(heads):
            at = group * heads + h
            columns_ref[:, at * PAIR : (at + 1) * PAIR] = w_ref[:, h * SLOT + PAIR : (h + 1) * SLOT]


def cuts(length):
    return [slice(c, c + CLUSTER) for c in range(0, length, CLUSTER)]


def attend(
    x_ref, weights, packs, order_ref, turned_ref, fields_ref, probs_ref, ctx_ref,
    place_ref, position_ref, raw_ref, scores_ref, columns_ref,
):
    length = x_ref.shape[0]
    heads = weights[0].shape[1] // SLOT
    count = 2 * heads
    lanes = lax.broadcasted_iota(jnp.int32, (length, SLOT), 1)
    bias_row = packs[0].shape[0] - 2
    for group, (w_ref, pack) in enumerate(zip(weights, packs)):
        bias = jnp.concatenate([pack[bias_row : bias_row + 1, :], pack[bias_row + 1 : bias_row + 2, :]], axis=1)
        for h in range(heads):
            fields = mm(x_ref[...], w_ref[:, h * SLOT : (h + 1) * SLOT]) + bias[:, h * SLOT : (h + 1) * SLOT]
            raw_ref[group * heads + h] = jnp.where(lanes < 3 * HEAD_DIM, fields, turned_ref[:, count : count + 1]).astype(BF16)
    put_tables(order_ref, turned_ref, count, place_ref, position_ref)
    order_low = order_ref[...].astype(BF16)
    seg_rows = []
    for at in range(count):
        fields_ref[at] = mm(place_ref[at], raw_ref[at]).astype(BF16)
        seg_rows.append(mm(order_low, position_ref[at])[count : count + 1, :])
    for at in range(count):
        for c, cut in enumerate(cuts(length)):
            seg_col = fields_ref[at, cut, SLOT - PAIR : SLOT].astype(F32)[:, PAIR - 1 : PAIR]
            scores = mm_nt(fields_ref[at, cut, 0:HEAD_DIM], fields_ref[at, cut, PAIR : PAIR + HEAD_DIM]) * SCALE
            scores_ref[at, cut, :] = jnp.where(seg_col == seg_rows[at][:, cut], scores, MASKED)
    for at in range(count):
        for cut in cuts(length):
            scores = scores_ref[at, cut, :]
            raised = jnp.exp(scores - jnp.max(scores, axis=-1, keepdims=True))
            probs_ref[at, cut, :] = (raised / jnp.sum(raised, axis=-1, keepdims=True)).astype(BF16)
    low_lanes = lax.broadcasted_iota(jnp.int32, (CLUSTER, PAIR), 1) < HEAD_DIM
    for at in range(count):
        for cut in cuts(length):
            mixed = mm(probs_ref[at, cut, :], fields_ref[at, cut, 0:PAIR])
            raw_ref[at, cut, 0:PAIR] = jnp.where(low_lanes, 0.0, mixed).astype(BF16)
    for at in range(count):
        ctx_ref[:, at * PAIR : (at + 1) * PAIR] = mm(position_ref[at], raw_ref[at, :, 0:PAIR]).astype(BF16)
    put_out_columns(weights, columns_ref)


def near_attention(
    where_ref, x_ref, w0_ref, w1_ref, pack0_ref, pack1_ref, seg_ref,
    fields_ref, probs_ref, ctx_ref, sum_ref, order_ref, turned_ref,
    place_ref, position_ref, raw_ref, scores_ref, columns_ref,
):
    packs = (pack0_ref, pack1_ref)
    put_orders(where_ref, packs, seg_ref, order_ref, turned_ref)
    attend(
        x_ref, (w0_ref, w1_ref), packs, order_ref, turned_ref, fields_ref, probs_ref, ctx_ref,
        place_ref, position_ref, raw_ref, scores_ref, columns_ref,
    )
    sum_ref[...] = mm_nt(ctx_ref[...], columns_ref[...])


def blocks(length):
    return [slice(r, r + BLOCK) for r in range(0, length, BLOCK)]


def far_attention(
    where_ref, x_ref, a2_ref, b2_ref, a3_ref, b3_ref, pack2_ref, pack3_ref, seg_ref, sum_ref, vec_ref,
    fields_ref, probs_ref, ctx_ref, order_ref, turned_ref, low_ref, normed_ref, inverse_ref,
    place_ref, position_ref, raw_ref, scores_ref, columns_ref, w2_ref, w3_ref, total_ref,
):
    packs = (pack2_ref, pack3_ref)
    assemble(w2_ref, a2_ref, b2_ref, where_ref[0])
    assemble(w3_ref, a3_ref, b3_ref, where_ref[0])
    put_orders(where_ref, packs, seg_ref, order_ref, turned_ref)
    attend(
        x_ref, (w2_ref, w3_ref), packs, order_ref, turned_ref, fields_ref, probs_ref, ctx_ref,
        place_ref, position_ref, raw_ref, scores_ref, columns_ref,
    )
    total_ref[...] = mm_nt(ctx_ref[...], columns_ref[...])
    for r in blocks(x_ref.shape[0]):
        normed, inverse = norm(x_ref[r, :].astype(F32) + sum_ref[r, :] + total_ref[r, :] + vec_ref[0:1, :])
        low_ref[r, :] = (normed * vec_ref[1:2, :] + vec_ref[2:3, :]).astype(BF16)
        normed_ref[r, :] = normed
        inverse_ref[r, :] = inverse


def up_bias(pack_ref, width):
    row = pack_ref.shape[0] - 4
    return jnp.concatenate([pack_ref[row : row + 1, :], pack_ref[row + 1 : row + 2, :]], axis=1)[:, 0:width]


def hidden_units(low_ref, up_ref, shift, hidden_ref, slope_ref):
    length = low_ref.shape[0]
    for r in blocks(length):
        v = mm(low_ref[r, :], up_ref[...]) + shift
        half = 0.5 + 0.5 * lax.erf(v * ROOT_HALF)
        hidden_ref[r, :] = (v * half).astype(BF16)
        slope_ref[r, :] = (half + v * jnp.exp(-0.5 * v * v) * INV_ROOT_TWO_PI).astype(BF16)


def near_forward(low_ref, u0_ref, u1_ref, d0_ref, d1_ref, pack0_ref, pack1_ref, hidden_ref, slope_ref, sum_ref):
    width = u0_ref.shape[1]
    hidden_units(low_ref, u0_ref, up_bias(pack0_ref, width), hidden_ref.at[0], slope_ref.at[0])
    hidden_units(low_ref, u1_ref, up_bias(pack1_ref, width), hidden_ref.at[1], slope_ref.at[1])
    for r in blocks(low_ref.shape[0]):
        sum_ref[r, :] = mm(hidden_ref[0, r, :], d0_ref[...]) + mm(hidden_ref[1, r, :], d1_ref[...])


def far_up(where_ref, low_ref, a2_ref, b2_ref, a3_ref, b3_ref, pack2_ref, pack3_ref, hidden_ref, slope_ref, u2_ref, u3_ref):
    width = a2_ref.shape[1]
    assemble(u2_ref, a2_ref, b2_ref, where_ref[0])
    assemble(u3_ref, a3_ref, b3_ref, where_ref[0])
    hidden_units(low_ref, u2_ref, up_bias(pack2_ref, width), hidden_ref.at[0], slope_ref.at[0])
    hidden_units(low_ref, u3_ref, up_bias(pack3_ref, width), hidden_ref.at[1], slope_ref.at[1])


def far_down(
    where_ref, hidden_ref, a2_ref, b2_ref, a3_ref, b3_ref, sum_ref, normed_a_ref, cot_ref, vec_ref,
    out_ref, grad_ref, grad_low_ref, sums_ref, d2_ref, d3_ref,
):
    assemble(d2_ref, a2_ref, b2_ref, where_ref[0])
    assemble(d3_ref, a3_ref, b3_ref, where_ref[0])
    sums_ref[...] = jnp.zeros_like(sums_ref)
    for r in blocks(hidden_ref.shape[1]):
        total = sum_ref[r, :] + mm(hidden_ref[0, r, :], d2_ref[...]) + mm(hidden_ref[1, r, :], d3_ref[...])
        middle = normed_a_ref[r, :] * vec_ref[1:2, :] + vec_ref[2:3, :]
        normed, inverse = norm(middle + total + vec_ref[3:4, :])
        out_ref[r, :] = (normed * vec_ref[4:5, :] + vec_ref[5:6, :]).astype(BF16)
        cot = cot_ref[r, :].astype(F32)
        grad = norm_back(cot, normed, inverse, vec_ref[4:5, :])
        grad_ref[r, :] = grad
        grad_low_ref[r, :] = grad.astype(BF16)
        sums_ref[0:1, :] += colsum(cot * normed)
        sums_ref[1:2, :] += colsum(cot)
        sums_ref[2:3, :] += colsum(grad)


def down_grads(far_ref, near_ref, grad_low_ref, g3_ref, g2_ref, g1_ref, g0_ref):
    g3_ref[...] = mm_tn(far_ref[1], grad_low_ref[...]).astype(BF16)
    g2_ref[...] = mm_tn(far_ref[0], grad_low_ref[...]).astype(BF16)
    g1_ref[...] = mm_tn(near_ref[1], grad_low_ref[...]).astype(BF16)
    g0_ref[...] = mm_tn(near_ref[0], grad_low_ref[...]).astype(BF16)


def up_grads(grad_low_ref, low_ref, slope_ref, down_ref, up_ref, pre_ref, out_ref, mid_ref, first, sums_ref, at):
    pre = (mm_nt(grad_low_ref[...], down_ref[...]) * slope_ref[...].astype(F32)).astype(BF16)
    pre_ref[...] = pre
    sums_ref[at : at + 1, :] = colsum(pre.astype(F32))
    out_ref[...] = mm_tn(low_ref[...], pre_ref[...]).astype(BF16)
    part = mm_nt(pre_ref[...], up_ref[...])
    mid_ref[...] = part if first else mid_ref[...] + part


def far_up_grads(
    where_ref, grad_low_ref, low_ref, slope_ref, d2a_ref, d2b_ref, d3a_ref, d3b_ref, u2a_ref, u2b_ref, u3a_ref, u3b_ref,
    g3_ref, g2_ref, mid_ref, shift_ref, d2_ref, d3_ref, u2_ref, u3_ref, pre2_ref, pre3_ref,
):
    side = where_ref[0]
    shift_ref[...] = jnp.zeros_like(shift_ref)
    assemble(d3_ref, d3a_ref, d3b_ref, side)
    assemble(u3_ref, u3a_ref, u3b_ref, side)
    assemble(d2_ref, d2a_ref, d2b_ref, side)
    assemble(u2_ref, u2a_ref, u2b_ref, side)
    up_grads(grad_low_ref, low_ref, slope_ref.at[1], d3_ref, u3_ref, pre3_ref, g3_ref, mid_ref, True, shift_ref, 1)
    up_grads(grad_low_ref, low_ref, slope_ref.at[0], d2_ref, u2_ref, pre2_ref, g2_ref, mid_ref, False, shift_ref, 0)


def near_up_grads(
    grad_low_ref, low_ref, slope_ref, d0_ref, d1_ref, u0_ref, u1_ref, far_mid_ref, grad_b_ref, normed_ref, inverse_ref,
    vec_ref, g1_ref, g0_ref, grad_ref, grad_out_ref, shift_ref, sums_ref, pre0_ref, pre1_ref, mid_ref,
):
    shift_ref[...] = jnp.zeros_like(shift_ref)
    sums_ref[...] = jnp.zeros_like(sums_ref)
    up_grads(grad_low_ref, low_ref, slope_ref.at[1], d1_ref, u1_ref, pre1_ref, g1_ref, mid_ref, True, shift_ref, 1)
    up_grads(grad_low_ref, low_ref, slope_ref.at[0], d0_ref, u0_ref, pre0_ref, g0_ref, mid_ref, False, shift_ref, 0)
    for r in blocks(low_ref.shape[0]):
        total = mid_ref[r, :] + far_mid_ref[r, :] + grad_b_ref[r, :]
        normed = normed_ref[r, :]
        grad = norm_back(total, normed, inverse_ref[r, :], vec_ref[1:2, :])
        grad_ref[r, :] = grad
        grad_out_ref[r, :] = grad.astype(BF16)
        sums_ref[0:1, :] += colsum(total * normed)
        sums_ref[1:2, :] += colsum(total)
        sums_ref[2:3, :] += colsum(grad)


def attend_back(
    x_ref, grad_out_ref, weights, order_ref, turned_ref, fields_ref, probs_ref, ctx_ref, outs,
    sums_b_ref, sums_a_ref, shift_ref, place_ref, position_ref, columns_ref, grads_ref, moved_ref, raw_ref, tok_ref, scores_ref, low_ref,
):
    length, width = x_ref.shape
    heads = weights[0].shape[1] // SLOT
    count = 2 * heads
    put_tables(order_ref, turned_ref, count, place_ref, position_ref)
    put_out_columns(weights, columns_ref)
    grads_ref[...] = mm(grad_out_ref[...], columns_ref[...]).astype(BF16)
    for at in range(count):
        moved_ref[at] = mm(place_ref[at], grads_ref[:, at * PAIR : (at + 1) * PAIR]).astype(BF16)
    low_lanes = lax.broadcasted_iota(jnp.int32, (CLUSTER, PAIR), 1) < HEAD_DIM
    no_low = jnp.zeros((CLUSTER, PAIR), BF16)
    for at in range(count):
        for cut in cuts(length):
            values = jnp.where(low_lanes, no_low, fields_ref[at, cut, 0:PAIR])
            scores_ref[at, cut, :] = mm_nt(moved_ref[at, cut, :], values)
    for at in range(count):
        for cut in cuts(length):
            grad_probs = scores_ref[at, cut, :]
            probs = probs_ref[at, cut, :].astype(F32)
            delta = jnp.sum(grad_probs * probs, axis=-1, keepdims=True)
            low_ref[at, cut, :] = (probs * (grad_probs - delta)).astype(BF16)
    for at in range(count):
        for cut in cuts(length):
            grad_queries = mm(low_ref[at, cut, :], fields_ref[at, cut, PAIR:SLOT]) * SCALE
            grad_values = mm_tn(probs_ref[at, cut, :], moved_ref[at, cut, :])
            raw_ref[at, cut, 0:PAIR] = jnp.where(low_lanes, grad_queries, grad_values).astype(BF16)
    for at in range(count):
        for cut in cuts(length):
            grad_keys = mm_tn(low_ref[at, cut, :], fields_ref[at, cut, 0:PAIR]) * SCALE
            raw_ref[at, cut, PAIR:SLOT] = jnp.where(low_lanes, grad_keys, 0.0).astype(BF16)
    for group, out_ref in reversed(list(enumerate(outs))):
        for h in range(heads):
            at = group * heads + h
            tok_ref[group, :, h * SLOT : (h + 1) * SLOT] = mm(position_ref[at], raw_ref[at]).astype(BF16)
        out_grad = mm_tn(grad_out_ref[...], ctx_ref[:, group * heads * PAIR : (group + 1) * heads * PAIR])
        grad = mm_tn(x_ref[...], tok_ref[group])
        for h in range(heads):
            out_ref[0:width, h * SLOT : h * SLOT + PAIR] = grad[:, h * SLOT : h * SLOT + PAIR].astype(BF16)
            out_ref[0:width, h * SLOT + PAIR : (h + 1) * SLOT] = (
                grad[:, h * SLOT + PAIR : (h + 1) * SLOT] + out_grad[:, h * PAIR : (h + 1) * PAIR]
            ).astype(BF16)
        fields = colsum(tok_ref[group].astype(F32))
        block = jnp.concatenate([sums_b_ref[0:3, :], sums_a_ref[0:3, :], shift_ref[group : group + 1, :], fields], axis=0)
        zero = jnp.zeros((EXTRA - 8, width), F32)
        out_ref[width:, :] = jnp.concatenate([block, zero], axis=0).astype(BF16)


def far_attention_grads(
    where_ref, x_ref, grad_out_ref, a2_ref, b2_ref, a3_ref, b3_ref, order_ref, turned_ref, fields_ref, probs_ref, ctx_ref,
    sums_b_ref, sums_a_ref, shift_ref, g3_ref, g2_ref, sum_ref,
    place_ref, position_ref, columns_ref, grads_ref, moved_ref, raw_ref, tok_ref, scores_ref, low_ref, w2_ref, w3_ref,
):
    assemble(w2_ref, a2_ref, b2_ref, where_ref[0])
    assemble(w3_ref, a3_ref, b3_ref, where_ref[0])
    attend_back(
        x_ref, grad_out_ref, (w2_ref, w3_ref), order_ref, turned_ref, fields_ref, probs_ref, ctx_ref, (g2_ref, g3_ref),
        sums_b_ref, sums_a_ref, shift_ref, place_ref, position_ref, columns_ref, grads_ref, moved_ref, raw_ref, tok_ref, scores_ref, low_ref,
    )
    sum_ref[...] = mm_nt(tok_ref[0], w2_ref[...]) + mm_nt(tok_ref[1], w3_ref[...])


def near_attention_grads(
    x_ref, grad_out_ref, w0_ref, w1_ref, order_ref, turned_ref, fields_ref, probs_ref, ctx_ref,
    sums_b_ref, sums_a_ref, shift_ref, sum_ref, grad_a_ref, g1_ref, g0_ref, in_ref,
    place_ref, position_ref, columns_ref, grads_ref, moved_ref, raw_ref, tok_ref, scores_ref, low_ref,
):
    attend_back(
        x_ref, grad_out_ref, (w0_ref, w1_ref), order_ref, turned_ref, fields_ref, probs_ref, ctx_ref, (g0_ref, g1_ref),
        sums_b_ref, sums_a_ref, shift_ref, place_ref, position_ref, columns_ref, grads_ref, moved_ref, raw_ref, tok_ref, scores_ref, low_ref,
    )
    in_ref[...] = (mm_nt(tok_ref[0], w0_ref[...]) + mm_nt(tok_ref[1], w1_ref[...]) + sum_ref[...] + grad_a_ref[...]).astype(BF16)


def solution(mesh):
    dp_size, tensor_size = mesh.shape["dp"], mesh.shape["tensor"]
    levels = dp_size.bit_length() - 1

    def swap(v, axis, bit):
        size = tensor_size if axis == "tensor" else dp_size
        return lax.ppermute(v, axis, [(i, i ^ (1 << bit)) for i in range(size)])

    def core_swap(v):
        return swap(v, "tensor", 0)

    def chip_swap(v):
        return swap(v, "tensor", 1)

    def add(a, b):
        return lax.reduce_precision(a.astype(F32) + b.astype(F32), 8, 7).astype(BF16)

    def on_device(
        layer_input, out_cotangent, qkv_weight, qv_bias, out_weight, out_bias, norm1_gain, norm1_bias,
        up_weight, up_bias, down_weight, down_bias, norm2_gain, norm2_bias, cluster_perm, segment_ids,
    ):
        length, width = layer_input.shape
        seqs, heads, _ = cluster_perm.shape
        units = up_weight.shape[1]
        mine = lax.axis_index("tensor")
        place = lax.axis_index("dp")
        side = place & 1
        half = width // 2

        where_arg = jnp.stack([side, mine]).astype(jnp.int32)
        count = 2 * heads
        lines = jnp.concatenate(
            [out_bias, norm1_gain, norm1_bias, down_bias, norm2_gain, norm2_bias, up_bias, qv_bias.reshape(-1),
             jnp.zeros((2 * width - units - 2 * heads * HEAD_DIM,), BF16)]
        ).reshape(8, width)
        square, half_t = ((width, width), BF16), ((half, width), BF16)
        vec_t = ((8, width), F32)
        small_t = ((seqs * heads + 4, length), F32)
        packed, packed_half, small, vecs = call(
            prepare, [square, half_t, small_t, vec_t], [], 3, where_arg, qkv_weight, out_weight, cluster_perm, lines
        )

        def own_half(m):
            return lax.dynamic_slice_in_dim(m, side * half, half, axis=0)

        def gather(m, m_half):
            first = chip_swap(m_half)
            second = swap(first, "dp", 0)
            return core_swap(m), (first, second, core_swap(first), core_swap(second))

        small_2, small_1 = chip_swap(small), core_swap(small)
        halves = [packed_half, own_half(up_weight), own_half(down_weight)]
        c_first, u_first, d_first = [chip_swap(m) for m in halves]
        c1, u1, d1 = core_swap(packed), core_swap(up_weight), core_swap(down_weight)

        def relay(first):
            second = swap(first, "dp", 0)
            return first, second, core_swap(first), second

        fields_t = ((count, length, SLOT), BF16)
        probs_t = ((count, length, CLUSTER), BF16)
        ctx_t = ((length, count * PAIR), BF16)
        orders_t = [((8, length), F32), ((length, 8), F32)]
        rows_f, rows_b = ((length, width), F32), ((length, width), BF16)
        pair_b = ((2, length, units), BF16)
        tall = ((width + EXTRA, heads * SLOT), BF16)
        mat, rows_s = pltpu.VMEM((width, width), BF16), pltpu.VMEM((length, width), BF16)
        tables = [pltpu.VMEM((count, length, length), BF16)] * 2
        columns = pltpu.VMEM((width, count * PAIR), BF16)
        raw = pltpu.VMEM((count, length, SLOT), BF16)
        scores = pltpu.VMEM((count, length, CLUSTER), F32)
        back = tables + [columns, rows_s, pltpu.VMEM((count, length, PAIR), BF16), raw, pltpu.VMEM((2, length, width), BF16)]
        back += [scores, pltpu.VMEM((count, length, CLUSTER), BF16)]

        near_fields, near_probs, near_ctx, attn_sum, *near_orders = call(
            near_attention, [fields_t, probs_t, ctx_t, rows_f, *orders_t], [*tables, raw, scores, columns], 8,
            where_arg, layer_input, packed, c1, small, small_1, segment_ids, after=(small_2,),
        )
        small_3 = core_swap(small_2)
        c_far = relay(tie(c_first, attn_sum))
        c_far = (*c_far[:3], core_swap(c_far[3]))
        u_far = relay(tie(u_first, attn_sum))
        far_fields, far_probs, far_ctx, *far_orders, low, normed_a, inverse_a = call(
            far_attention, [fields_t, probs_t, ctx_t, *orders_t, rows_b, rows_f, ((length, 1), F32)],
            [*tables, raw, scores, columns, mat, mat, pltpu.VMEM((length, width), F32)], 1,
            where_arg, layer_input, *c_far, small_2, small_3, segment_ids, attn_sum, vecs,
        )
        u_far = (*u_far[:3], core_swap(tie(u_far[3], low)))
        d_far = relay(tie(d_first, low))
        near_hidden, near_slope, ffn_sum = call(
            near_forward, [pair_b, pair_b, rows_f], [], 6, low, up_weight, u1, down_weight, d1, small, small_1
        )
        far_hidden, far_slope = call(
            far_up, [pair_b, pair_b], [mat, mat], 5, where_arg, low, *u_far, small_2, small_3
        )
        d_far = (*d_far[:3], core_swap(tie(d_far[3], ffn_sum, far_hidden)))
        layer_output, grad_b, grad_b_low, sums_b = call(
            far_down, [rows_b, rows_f, rows_b, vec_t], [mat, mat], 5,
            where_arg, far_hidden, *d_far, ffn_sum, normed_a, out_cotangent, vecs,
        )
        dg3, dg2, dg1, dg0 = call(down_grads, [square] * 4, [], 2.8, far_hidden, near_hidden, grad_b_low)
        ds3, ds1 = core_swap(dg3), core_swap(dg1)
        ug3, ug2, grad_mid, far_ub = call(
            far_up_grads, [square, square, rows_f, vec_t], [mat] * 4 + [rows_s] * 2, 0.1,
            where_arg, grad_b_low, low, far_slope, *d_far, *u_far,
        )
        us3 = core_swap(ug3)
        down_cross = add(dg2, tie(ds3, grad_mid))
        ug1, ug0, grad_a, grad_a_low, near_ub, sums_a = call(
            near_up_grads, [square, square, rows_f, rows_b, vec_t, vec_t], [rows_s, rows_s, pltpu.VMEM((length, width), F32)], 0.1,
            grad_b_low, low, near_slope, down_weight, d1, up_weight, u1, grad_mid, grad_b, normed_a, inverse_a, vecs,
            after=(down_cross,),
        )
        us1 = core_swap(ug1)
        up_cross = add(ug2, tie(us3, grad_a_low))
        cg3, cg2, in_sum = call(
            far_attention_grads, [tall, tall, rows_f], back + [mat, mat], 0.1,
            where_arg, layer_input, grad_a_low, *c_far, *far_orders, far_fields, far_probs, far_ctx, sums_b, sums_a, far_ub,
            after=(up_cross,),
        )
        cs3 = core_swap(cg3)
        down_total = add(add(dg0, ds1), tie(chip_swap(down_cross), in_sum))
        packed_cross = add(cg2, cs3)
        cg1, cg0, input_grad = call(
            near_attention_grads, [tall, tall, rows_b], back, 0.1,
            layer_input, grad_a_low, packed, c1, *near_orders, near_fields, near_probs, near_ctx,
            sums_b, sums_a, near_ub, in_sum, grad_a, after=(down_total, packed_cross),
        )
        steps = [(level, True) for level in range(levels)] + [(level, False) for level in reversed(range(levels))]

        def step(total, at, *others):
            level, halve = steps[at]
            bit = (place >> level) & 1
            if halve:
                rows = total.shape[0] // 2
                send = lax.dynamic_slice_in_dim(total, (1 - bit) * rows, rows, axis=0)
                keep = lax.dynamic_slice_in_dim(total, bit * rows, rows, axis=0)
                return add(keep, tie(swap(send, "dp", level), *others))
            other = tie(swap(total, "dp", level), *others)
            return jnp.where(
                bit == 0, jnp.concatenate([total, other], axis=0), jnp.concatenate([other, total], axis=0)
            )

        last = len(steps) - 1
        down, up, whole = [down_total], [], []

        def reach(chain, at, *others):
            while len(chain) < min(at, last) + 2:
                chain.append(step(chain[-1], len(chain) - 1, *others))
            return chain[-1]

        reach(down, 0, input_grad)
        up.append(add(add(ug0, us1), tie(chip_swap(up_cross), down[-1])))
        reach(down, 2)
        reach(up, 0, down[-1])
        reach(down, 3, up[-1])
        whole.append(add(add(cg0, core_swap(cg1)), tie(chip_swap(packed_cross), down[-1], up[-1])))
        for at in range(last + 1):
            reach(down, max(4, at + 3))
            reach(up, at + 2 - (at > 1))
            reach(whole, at, down[-1], up[-1])
        down_grad, up_grad = [tie(chain[-1], whole[-2]).astype(F32) for chain in (down, up)]
        packed_grad = whole[-1]
        qkv_grad, out_grad, sums, qv_grad = call(
            unpack,
            [((3, heads * HEAD_DIM, width), F32), ((heads * HEAD_DIM, width), F32), ((16, width), F32),
             ((2, heads * HEAD_DIM), F32)],
            [pltpu.VMEM((3, heads * HEAD_DIM, width), F32), pltpu.SemaphoreType.DMA((3,))], 1, packed_grad, apart=1,
        )
        return (
            layer_output, input_grad, qkv_grad.transpose(0, 2, 1), qv_grad, out_grad, sums[5], sums[3], sums[4],
            up_grad, sums[6], down_grad, sums[2], sums[0], sums[1],
        )

    rows, split, copied = P(("dp", "tensor"), None), P(None, "tensor"), P()
    in_specs = (
        rows, rows, P(None, None, "tensor"), split, P("tensor", None), copied, copied, copied, split, P("tensor"),
        P("tensor", None), copied, copied, copied, P("dp", "tensor", None), P("dp", None),
    )
    out_specs = (
        rows, rows, P(None, None, "tensor"), split, P("tensor", None), copied, copied, copied, split, P("tensor"),
        P("tensor", None), copied, copied, copied,
    )
    return jax.shard_map(on_device, mesh=mesh, in_specs=in_specs, out_specs=out_specs, check_vma=False)
```

```python
import math

import jax
import jax.numpy as jnp
from jax import lax
from jax.experimental import pallas as pl
from jax.experimental.pallas import tpu as pltpu
from jax.sharding import PartitionSpec as P

HEAD_DIM = 64
CLUSTER = 128
NORM_EPS = 1e-12
MASKED = -1000000000.0
ROOT_HALF = 0.7071067811865476
INV_ROOT_TWO_PI = 0.3989422804014327
SCALE = 1.0 / math.sqrt(HEAD_DIM)
SLOT = 4 * HEAD_DIM
PAIR = 2 * HEAD_DIM
BLOCK = 128
VMEM_LIMIT = 30 * 1024 * 1024
EXTRA = 32
F32 = jnp.float32
BF16 = jnp.bfloat16


def mm(a, b):
    return jnp.dot(a, b, preferred_element_type=F32)


def mm_nt(a, b):
    return lax.dot_general(a, b, (((1,), (1,)), ((), ())), preferred_element_type=F32)


def mm_tn(a, b):
    return lax.dot_general(a, b, (((0,), (0,)), ((), ())), preferred_element_type=F32)


def call(body, outs, scratch, micros, *args, after=(), apart=0):
    shapes = [jax.ShapeDtypeStruct(s, t) for s, t in outs]
    kept = len(args)

    def placed(a):
        flat = a.ndim == 1 and a.dtype == jnp.int32
        return pl.BlockSpec(memory_space=pltpu.SMEM if flat else pltpu.VMEM)

    def run(*refs):
        body(*refs[:kept], *refs[kept + len(after) :])

    return pl.pallas_call(
        run,
        out_shape=shapes,
        in_specs=[placed(a) for a in args] + [pl.BlockSpec(memory_space=pl.ANY)] * len(after),
        out_specs=[pl.BlockSpec(memory_space=pltpu.HBM if i < apart else pltpu.VMEM) for i in range(len(outs))],
        scratch_shapes=scratch,
        cost_estimate=pl.CostEstimate(flops=int(micros * 1e9), bytes_accessed=0, transcendentals=0),
        compiler_params=pltpu.CompilerParams(vmem_limit_bytes=VMEM_LIMIT),
    )(*args, *after)


def tie(value, *others):
    return lax.optimization_barrier((value, *others))[0]


def norm(values):
    center = values - jnp.mean(values, axis=-1, keepdims=True)
    inverse = lax.rsqrt(jnp.mean(center * center, axis=-1, keepdims=True) + NORM_EPS)
    return center * inverse, inverse


def norm_back(grad_in, normed, inverse, gain):
    scaled = grad_in * gain
    return inverse * (
        scaled
        - jnp.mean(scaled, axis=-1, keepdims=True)
        - normed * jnp.mean(scaled * normed, axis=-1, keepdims=True)
    )


def colsum(v):
    return jnp.sum(v, axis=0, keepdims=True)


def assemble(scratch, half_ref, relayed_ref, side):
    rows = half_ref.shape[0]
    here, there = half_ref[...], relayed_ref[...]
    scratch[0:rows, :] = jnp.where(side == 0, here, there)
    scratch[rows : 2 * rows, :] = jnp.where(side == 0, there, here)


def prepare(where_ref, qkv_ref, out_ref, perm_ref, vec_ref, packed_ref, half_ref, small_ref, lines_ref):
    width = qkv_ref.shape[1]
    turned = out_ref[...].astype(F32).T.astype(BF16)
    heads = qkv_ref.shape[2] // HEAD_DIM
    for h in range(heads):
        cut = slice(h * HEAD_DIM, (h + 1) * HEAD_DIM)
        packed_ref[:, h * SLOT : (h + 1) * SLOT] = jnp.concatenate(
            [qkv_ref[0, :, cut], qkv_ref[2, :, cut], qkv_ref[1, :, cut], turned[:, cut]], axis=1
        )
    half = width // 2
    half_ref[...] = jnp.where(where_ref[0] == 0, packed_ref[0:half, :], packed_ref[half:width, :])
    lines = vec_ref[...].astype(F32)
    lines_ref[...] = lines
    seqs = perm_ref.shape[0]
    for s in range(seqs):
        small_ref[s * heads : (s + 1) * heads, :] = perm_ref[s].astype(F32)
    own = heads * HEAD_DIM
    blank = jnp.zeros((1, 2 * HEAD_DIM), F32)
    bias = []
    for h in range(heads):
        bias += [lines[7:8, h * HEAD_DIM : (h + 1) * HEAD_DIM], lines[7:8, own + h * HEAD_DIM : own + (h + 1) * HEAD_DIM], blank]
    length = small_ref.shape[1]
    for row, line in ((seqs * heads, lines[6:7, :]), (seqs * heads + 2, jnp.concatenate(bias, axis=1))):
        small_ref[row : row + 1, :] = line[:, 0:length]
        rest = line.shape[1] - length
        small_ref[row + 1 : row + 2, :] = jnp.concatenate([line[:, length:], jnp.zeros((1, length - rest), F32)], axis=1)


def unpack(packed_ref, qkv_out_ref, out_ref, vec_ref, bias_ref, qkv_ref, sems):
    width = packed_ref.shape[1]
    heads = width // SLOT
    rows = qkv_ref.shape[2]

    def field(at):
        return jnp.concatenate(
            [packed_ref[0:rows, h * SLOT + at * HEAD_DIM : h * SLOT + (at + 1) * HEAD_DIM] for h in range(heads)], axis=1
        ).astype(F32)

    copies = []
    for at, member in enumerate((0, 2, 1)):
        qkv_ref[member] = field(at).T
        copies.append(pltpu.make_async_copy(qkv_ref.at[member], qkv_out_ref.at[member], sems.at[at]))
        copies[-1].start()
    out_ref[...] = field(3).T
    vectors = packed_ref[rows : rows + 16, :].astype(F32)
    vec_ref[...] = vectors
    for member in range(2):
        starts = [h * SLOT + member * HEAD_DIM for h in range(heads)]
        bias_ref[member : member + 1, :] = jnp.concatenate([vectors[7:8, c : c + HEAD_DIM] for c in starts], axis=1)
    for copy in copies:
        copy.wait()


def put_orders(where_ref, packs, seg_ref, order_ref, turned_ref):
    heads = order_ref.shape[0] // 2 - 1
    order_ref[...] = jnp.zeros_like(order_ref)
    for group, pack in enumerate(packs):
        for h in range(heads):
            at = group * heads + h
            order_ref[at : at + 1, :] = pack[pl.ds(where_ref[1] * heads + h, 1), :]
    order_ref[2 * heads : 2 * heads + 1, :] = seg_ref[pl.ds(where_ref[1], 1), :].astype(F32)
    turned_ref[...] = order_ref[...].T


def put_tables(order_ref, turned_ref, count, place_ref, position_ref):
    length = order_ref.shape[1]
    lane = lax.broadcasted_iota(jnp.int32, (length, length), 1).astype(F32)
    sub = lax.broadcasted_iota(jnp.int32, (length, length), 0).astype(F32)
    for at in range(count):
        place_ref[at] = jnp.where(turned_ref[:, at : at + 1] == lane, 1.0, 0.0).astype(BF16)
        position_ref[at] = jnp.where(order_ref[at : at + 1, :] == sub, 1.0, 0.0).astype(BF16)


def put_out_columns(weights, columns_ref):
    heads = weights[0].shape[1] // SLOT
    for group, w_ref in enumerate(weights):
        for h in range(heads):
            at = group * heads + h
            columns_ref[:, at * PAIR : (at + 1) * PAIR] = w_ref[:, h * SLOT + PAIR : (h + 1) * SLOT]


def cuts(length):
    return [slice(c, c + CLUSTER) for c in range(0, length, CLUSTER)]


def attend(
    x_ref, weights, packs, order_ref, turned_ref, fields_ref, probs_ref, ctx_ref,
    place_ref, position_ref, raw_ref, scores_ref, columns_ref,
):
    length = x_ref.shape[0]
    heads = weights[0].shape[1] // SLOT
    count = 2 * heads
    lanes = lax.broadcasted_iota(jnp.int32, (length, SLOT), 1)
    bias_row = packs[0].shape[0] - 2
    for group, (w_ref, pack) in enumerate(zip(weights, packs)):
        bias = jnp.concatenate([pack[bias_row : bias_row + 1, :], pack[bias_row + 1 : bias_row + 2, :]], axis=1)
        for h in range(heads):
            fields = mm(x_ref[...], w_ref[:, h * SLOT : (h + 1) * SLOT]) + bias[:, h * SLOT : (h + 1) * SLOT]
            raw_ref[group * heads + h] = jnp.where(lanes < 3 * HEAD_DIM, fields, turned_ref[:, count : count + 1]).astype(BF16)
    put_tables(order_ref, turned_ref, count, place_ref, position_ref)
    order_low = order_ref[...].astype(BF16)
    seg_rows = []
    for at in range(count):
        fields_ref[at] = mm(place_ref[at], raw_ref[at]).astype(BF16)
        seg_rows.append(mm(order_low, position_ref[at])[count : count + 1, :])
    for at in range(count):
        for c, cut in enumerate(cuts(length)):
            seg_col = fields_ref[at, cut, SLOT - PAIR : SLOT].astype(F32)[:, PAIR - 1 : PAIR]
            scores = mm_nt(fields_ref[at, cut, 0:HEAD_DIM], fields_ref[at, cut, PAIR : PAIR + HEAD_DIM]) * SCALE
            scores_ref[at, cut, :] = jnp.where(seg_col == seg_rows[at][:, cut], scores, MASKED)
    for at in range(count):
        for cut in cuts(length):
            scores = scores_ref[at, cut, :]
            raised = jnp.exp(scores - jnp.max(scores, axis=-1, keepdims=True))
            probs_ref[at, cut, :] = (raised / jnp.sum(raised, axis=-1, keepdims=True)).astype(BF16)
    low_lanes = lax.broadcasted_iota(jnp.int32, (CLUSTER, PAIR), 1) < HEAD_DIM
    for at in range(count):
        for cut in cuts(length):
            mixed = mm(probs_ref[at, cut, :], fields_ref[at, cut, 0:PAIR])
            raw_ref[at, cut, 0:PAIR] = jnp.where(low_lanes, 0.0, mixed).astype(BF16)
    for at in range(count):
        ctx_ref[:, at * PAIR : (at + 1) * PAIR] = mm(position_ref[at], raw_ref[at, :, 0:PAIR]).astype(BF16)
    put_out_columns(weights, columns_ref)


def near_attention(
    where_ref, x_ref, w0_ref, w1_ref, pack0_ref, pack1_ref, seg_ref,
    fields_ref, probs_ref, ctx_ref, sum_ref, order_ref, turned_ref,
    place_ref, position_ref, raw_ref, scores_ref, columns_ref,
):
    packs = (pack0_ref, pack1_ref)
    put_orders(where_ref, packs, seg_ref, order_ref, turned_ref)
    attend(
        x_ref, (w0_ref, w1_ref), packs, order_ref, turned_ref, fields_ref, probs_ref, ctx_ref,
        place_ref, position_ref, raw_ref, scores_ref, columns_ref,
    )
    sum_ref[...] = mm_nt(ctx_ref[...], columns_ref[...])


def blocks(length):
    return [slice(r, r + BLOCK) for r in range(0, length, BLOCK)]


def far_attention(
    where_ref, x_ref, a2_ref, b2_ref, a3_ref, b3_ref, pack2_ref, pack3_ref, seg_ref, sum_ref, vec_ref,
    fields_ref, probs_ref, ctx_ref, order_ref, turned_ref, low_ref, normed_ref, inverse_ref,
    place_ref, position_ref, raw_ref, scores_ref, columns_ref, w2_ref, w3_ref, total_ref,
):
    packs = (pack2_ref, pack3_ref)
    assemble(w2_ref, a2_ref, b2_ref, where_ref[0])
    assemble(w3_ref, a3_ref, b3_ref, where_ref[0])
    put_orders(where_ref, packs, seg_ref, order_ref, turned_ref)
    attend(
        x_ref, (w2_ref, w3_ref), packs, order_ref, turned_ref, fields_ref, probs_ref, ctx_ref,
        place_ref, position_ref, raw_ref, scores_ref, columns_ref,
    )
    total_ref[...] = mm_nt(ctx_ref[...], columns_ref[...])
    for r in blocks(x_ref.shape[0]):
        normed, inverse = norm(x_ref[r, :].astype(F32) + sum_ref[r, :] + total_ref[r, :] + vec_ref[0:1, :])
        low_ref[r, :] = (normed * vec_ref[1:2, :] + vec_ref[2:3, :]).astype(BF16)
        normed_ref[r, :] = normed
        inverse_ref[r, :] = inverse


def up_bias(pack_ref, width):
    row = pack_ref.shape[0] - 4
    return jnp.concatenate([pack_ref[row : row + 1, :], pack_ref[row + 1 : row + 2, :]], axis=1)[:, 0:width]


def hidden_units(low_ref, up_ref, shift, hidden_ref, slope_ref):
    length = low_ref.shape[0]
    for r in blocks(length):
        v = mm(low_ref[r, :], up_ref[...]) + shift
        half = 0.5 + 0.5 * lax.erf(v * ROOT_HALF)
        hidden_ref[r, :] = (v * half).astype(BF16)
        slope_ref[r, :] = (half + v * jnp.exp(-0.5 * v * v) * INV_ROOT_TWO_PI).astype(BF16)


def near_forward(low_ref, u0_ref, u1_ref, d0_ref, d1_ref, pack0_ref, pack1_ref, hidden_ref, slope_ref, sum_ref):
    width = u0_ref.shape[1]
    hidden_units(low_ref, u0_ref, up_bias(pack0_ref, width), hidden_ref.at[0], slope_ref.at[0])
    hidden_units(low_ref, u1_ref, up_bias(pack1_ref, width), hidden_ref.at[1], slope_ref.at[1])
    for r in blocks(low_ref.shape[0]):
        sum_ref[r, :] = mm(hidden_ref[0, r, :], d0_ref[...]) + mm(hidden_ref[1, r, :], d1_ref[...])


def far_up(where_ref, low_ref, a2_ref, b2_ref, a3_ref, b3_ref, pack2_ref, pack3_ref, hidden_ref, slope_ref, u2_ref, u3_ref):
    width = a2_ref.shape[1]
    assemble(u2_ref, a2_ref, b2_ref, where_ref[0])
    assemble(u3_ref, a3_ref, b3_ref, where_ref[0])
    hidden_units(low_ref, u2_ref, up_bias(pack2_ref, width), hidden_ref.at[0], slope_ref.at[0])
    hidden_units(low_ref, u3_ref, up_bias(pack3_ref, width), hidden_ref.at[1], slope_ref.at[1])


def far_down(
    where_ref, hidden_ref, a2_ref, b2_ref, a3_ref, b3_ref, sum_ref, normed_a_ref, cot_ref, vec_ref,
    out_ref, grad_ref, grad_low_ref, sums_ref, d2_ref, d3_ref,
):
    assemble(d2_ref, a2_ref, b2_ref, where_ref[0])
    assemble(d3_ref, a3_ref, b3_ref, where_ref[0])
    sums_ref[...] = jnp.zeros_like(sums_ref)
    for r in blocks(hidden_ref.shape[1]):
        total = sum_ref[r, :] + mm(hidden_ref[0, r, :], d2_ref[...]) + mm(hidden_ref[1, r, :], d3_ref[...])
        middle = normed_a_ref[r, :] * vec_ref[1:2, :] + vec_ref[2:3, :]
        normed, inverse = norm(middle + total + vec_ref[3:4, :])
        out_ref[r, :] = (normed * vec_ref[4:5, :] + vec_ref[5:6, :]).astype(BF16)
        cot = cot_ref[r, :].astype(F32)
        grad = norm_back(cot, normed, inverse, vec_ref[4:5, :])
        grad_ref[r, :] = grad
        grad_low_ref[r, :] = grad.astype(BF16)
        sums_ref[0:1, :] += colsum(cot * normed)
        sums_ref[1:2, :] += colsum(cot)
        sums_ref[2:3, :] += colsum(grad)


def down_grads(far_ref, near_ref, grad_low_ref, g3_ref, g2_ref, g1_ref, g0_ref):
    g3_ref[...] = mm_tn(far_ref[1], grad_low_ref[...]).astype(BF16)
    g2_ref[...] = mm_tn(far_ref[0], grad_low_ref[...]).astype(BF16)
    g1_ref[...] = mm_tn(near_ref[1], grad_low_ref[...]).astype(BF16)
    g0_ref[...] = mm_tn(near_ref[0], grad_low_ref[...]).astype(BF16)


def up_grads(grad_low_ref, low_ref, slope_ref, down_ref, up_ref, pre_ref, out_ref, mid_ref, first, sums_ref, at):
    pre = (mm_nt(grad_low_ref[...], down_ref[...]) * slope_ref[...].astype(F32)).astype(BF16)
    pre_ref[...] = pre
    sums_ref[at : at + 1, :] = colsum(pre.astype(F32))
    out_ref[...] = mm_tn(low_ref[...], pre_ref[...]).astype(BF16)
    part = mm_nt(pre_ref[...], up_ref[...])
    mid_ref[...] = part if first else mid_ref[...] + part


def far_up_grads(
    where_ref, grad_low_ref, low_ref, slope_ref, d2a_ref, d2b_ref, d3a_ref, d3b_ref, u2a_ref, u2b_ref, u3a_ref, u3b_ref,
    g3_ref, g2_ref, mid_ref, shift_ref, d2_ref, d3_ref, u2_ref, u3_ref, pre2_ref, pre3_ref,
):
    side = where_ref[0]
    shift_ref[...] = jnp.zeros_like(shift_ref)
    assemble(d3_ref, d3a_ref, d3b_ref, side)
    assemble(u3_ref, u3a_ref, u3b_ref, side)
    assemble(d2_ref, d2a_ref, d2b_ref, side)
    assemble(u2_ref, u2a_ref, u2b_ref, side)
    up_grads(grad_low_ref, low_ref, slope_ref.at[1], d3_ref, u3_ref, pre3_ref, g3_ref, mid_ref, True, shift_ref, 1)
    up_grads(grad_low_ref, low_ref, slope_ref.at[0], d2_ref, u2_ref, pre2_ref, g2_ref, mid_ref, False, shift_ref, 0)


def near_up_grads(
    grad_low_ref, low_ref, slope_ref, d0_ref, d1_ref, u0_ref, u1_ref, far_mid_ref, grad_b_ref, normed_ref, inverse_ref,
    vec_ref, g1_ref, g0_ref, grad_ref, grad_out_ref, shift_ref, sums_ref, pre0_ref, pre1_ref, mid_ref,
):
    shift_ref[...] = jnp.zeros_like(shift_ref)
    sums_ref[...] = jnp.zeros_like(sums_ref)
    up_grads(grad_low_ref, low_ref, slope_ref.at[1], d1_ref, u1_ref, pre1_ref, g1_ref, mid_ref, True, shift_ref, 1)
    up_grads(grad_low_ref, low_ref, slope_ref.at[0], d0_ref, u0_ref, pre0_ref, g0_ref, mid_ref, False, shift_ref, 0)
    for r in blocks(low_ref.shape[0]):
        total = mid_ref[r, :] + far_mid_ref[r, :] + grad_b_ref[r, :]
        normed = normed_ref[r, :]
        grad = norm_back(total, normed, inverse_ref[r, :], vec_ref[1:2, :])
        grad_ref[r, :] = grad
        grad_out_ref[r, :] = grad.astype(BF16)
        sums_ref[0:1, :] += colsum(total * normed)
        sums_ref[1:2, :] += colsum(total)
        sums_ref[2:3, :] += colsum(grad)


def attend_back(
    x_ref, grad_out_ref, weights, order_ref, turned_ref, fields_ref, probs_ref, ctx_ref, outs,
    sums_b_ref, sums_a_ref, shift_ref, place_ref, position_ref, columns_ref, grads_ref, moved_ref, raw_ref, tok_ref, scores_ref, low_ref,
):
    length, width = x_ref.shape
    heads = weights[0].shape[1] // SLOT
    count = 2 * heads
    put_tables(order_ref, turned_ref, count, place_ref, position_ref)
    put_out_columns(weights, columns_ref)
    grads_ref[...] = mm(grad_out_ref[...], columns_ref[...]).astype(BF16)
    for at in range(count):
        moved_ref[at] = mm(place_ref[at], grads_ref[:, at * PAIR : (at + 1) * PAIR]).astype(BF16)
    low_lanes = lax.broadcasted_iota(jnp.int32, (CLUSTER, PAIR), 1) < HEAD_DIM
    no_low = jnp.zeros((CLUSTER, PAIR), BF16)
    for at in range(count):
        for cut in cuts(length):
            values = jnp.where(low_lanes, no_low, fields_ref[at, cut, 0:PAIR])
            scores_ref[at, cut, :] = mm_nt(moved_ref[at, cut, :], values)
    for at in range(count):
        for cut in cuts(length):
            grad_probs = scores_ref[at, cut, :]
            probs = probs_ref[at, cut, :].astype(F32)
            delta = jnp.sum(grad_probs * probs, axis=-1, keepdims=True)
            low_ref[at, cut, :] = (probs * (grad_probs - delta)).astype(BF16)
    for at in range(count):
        for cut in cuts(length):
            grad_queries = mm(low_ref[at, cut, :], fields_ref[at, cut, PAIR:SLOT]) * SCALE
            grad_values = mm_tn(probs_ref[at, cut, :], moved_ref[at, cut, :])
            raw_ref[at, cut, 0:PAIR] = jnp.where(low_lanes, grad_queries, grad_values).astype(BF16)
    for at in range(count):
        for cut in cuts(length):
            grad_keys = mm_tn(low_ref[at, cut, :], fields_ref[at, cut, 0:PAIR]) * SCALE
            raw_ref[at, cut, PAIR:SLOT] = jnp.where(low_lanes, grad_keys, 0.0).astype(BF16)
    for group, out_ref in reversed(list(enumerate(outs))):
        for h in range(heads):
            at = group * heads + h
            tok_ref[group, :, h * SLOT : (h + 1) * SLOT] = mm(position_ref[at], raw_ref[at]).astype(BF16)
        out_grad = mm_tn(grad_out_ref[...], ctx_ref[:, group * heads * PAIR : (group + 1) * heads * PAIR])
        grad = mm_tn(x_ref[...], tok_ref[group])
        for h in range(heads):
            out_ref[0:width, h * SLOT : h * SLOT + PAIR] = grad[:, h * SLOT : h * SLOT + PAIR].astype(BF16)
            out_ref[0:width, h * SLOT + PAIR : (h + 1) * SLOT] = (
                grad[:, h * SLOT + PAIR : (h + 1) * SLOT] + out_grad[:, h * PAIR : (h + 1) * PAIR]
            ).astype(BF16)
        fields = colsum(tok_ref[group].astype(F32))
        block = jnp.concatenate([sums_b_ref[0:3, :], sums_a_ref[0:3, :], shift_ref[group : group + 1, :], fields], axis=0)
        zero = jnp.zeros((out_ref.shape[0] - width - 8, width), F32)
        out_ref[width:, :] = jnp.concatenate([block, zero], axis=0).astype(BF16)


def far_attention_grads(
    where_ref, x_ref, grad_out_ref, a2_ref, b2_ref, a3_ref, b3_ref, order_ref, turned_ref, fields_ref, probs_ref, ctx_ref,
    sums_b_ref, sums_a_ref, shift_ref, g3_ref, g2_ref, sum_ref,
    place_ref, position_ref, columns_ref, grads_ref, moved_ref, raw_ref, tok_ref, scores_ref, low_ref, w2_ref, w3_ref,
):
    assemble(w2_ref, a2_ref, b2_ref, where_ref[0])
    assemble(w3_ref, a3_ref, b3_ref, where_ref[0])
    attend_back(
        x_ref, grad_out_ref, (w2_ref, w3_ref), order_ref, turned_ref, fields_ref, probs_ref, ctx_ref, (g2_ref, g3_ref),
        sums_b_ref, sums_a_ref, shift_ref, place_ref, position_ref, columns_ref, grads_ref, moved_ref, raw_ref, tok_ref, scores_ref, low_ref,
    )
    sum_ref[...] = mm_nt(tok_ref[0], w2_ref[...]) + mm_nt(tok_ref[1], w3_ref[...])


def near_attention_grads(
    x_ref, grad_out_ref, w0_ref, w1_ref, order_ref, turned_ref, fields_ref, probs_ref, ctx_ref,
    sums_b_ref, sums_a_ref, shift_ref, sum_ref, grad_a_ref, g1_ref, g0_ref, in_ref,
    place_ref, position_ref, columns_ref, grads_ref, moved_ref, raw_ref, tok_ref, scores_ref, low_ref,
):
    attend_back(
        x_ref, grad_out_ref, (w0_ref, w1_ref), order_ref, turned_ref, fields_ref, probs_ref, ctx_ref, (g0_ref, g1_ref),
        sums_b_ref, sums_a_ref, shift_ref, place_ref, position_ref, columns_ref, grads_ref, moved_ref, raw_ref, tok_ref, scores_ref, low_ref,
    )
    in_ref[...] = (mm_nt(tok_ref[0], w0_ref[...]) + mm_nt(tok_ref[1], w1_ref[...]) + sum_ref[...] + grad_a_ref[...]).astype(BF16)


def solution(mesh):
    dp_size, tensor_size = mesh.shape["dp"], mesh.shape["tensor"]
    levels = dp_size.bit_length() - 1

    def swap(v, axis, bit):
        size = tensor_size if axis == "tensor" else dp_size
        return lax.ppermute(v, axis, [(i, i ^ (1 << bit)) for i in range(size)])

    def core_swap(v):
        return swap(v, "tensor", 0)

    def chip_swap(v):
        return swap(v, "tensor", 1)

    def add(a, b):
        return lax.reduce_precision(a.astype(F32) + b.astype(F32), 8, 7).astype(BF16)

    def on_device(
        layer_input, out_cotangent, qkv_weight, qv_bias, out_weight, out_bias, norm1_gain, norm1_bias,
        up_weight, up_bias, down_weight, down_bias, norm2_gain, norm2_bias, cluster_perm, segment_ids,
    ):
        length, width = layer_input.shape
        seqs, heads, _ = cluster_perm.shape
        units = up_weight.shape[1]
        mine = lax.axis_index("tensor")
        place = lax.axis_index("dp")
        side = place & 1
        half = width // 2

        where_arg = jnp.stack([side, mine]).astype(jnp.int32)
        count = 2 * heads
        lines = jnp.concatenate(
            [out_bias, norm1_gain, norm1_bias, down_bias, norm2_gain, norm2_bias, up_bias, qv_bias.reshape(-1),
             jnp.zeros((2 * width - units - 2 * heads * HEAD_DIM,), BF16)]
        ).reshape(8, width)
        square, half_t = ((width, width), BF16), ((half, width), BF16)
        vec_t = ((8, width), F32)
        small_t = ((seqs * heads + 4, length), F32)
        packed, packed_half, small, vecs = call(
            prepare, [square, half_t, small_t, vec_t], [], 3, where_arg, qkv_weight, out_weight, cluster_perm, lines
        )

        def own_half(m):
            return lax.dynamic_slice_in_dim(m, side * half, half, axis=0)

        def gather(m, m_half):
            first = chip_swap(m_half)
            second = swap(first, "dp", 0)
            return core_swap(m), (first, second, core_swap(first), core_swap(second))

        small_2, small_1 = chip_swap(small), core_swap(small)
        halves = [packed_half, own_half(up_weight), own_half(down_weight)]
        c_first, u_first, d_first = [chip_swap(m) for m in halves]
        c1, u1, d1 = core_swap(packed), core_swap(up_weight), core_swap(down_weight)

        def relay(first):
            second = swap(first, "dp", 0)
            return first, second, core_swap(first), second

        fields_t = ((count, length, SLOT), BF16)
        probs_t = ((count, length, CLUSTER), BF16)
        ctx_t = ((length, count * PAIR), BF16)
        orders_t = [((8, length), F32), ((length, 8), F32)]
        rows_f, rows_b = ((length, width), F32), ((length, width), BF16)
        pair_b = ((2, length, units), BF16)
        tall = ((width + max(EXTRA, dp_size), heads * SLOT), BF16)
        mat, rows_s = pltpu.VMEM((width, width), BF16), pltpu.VMEM((length, width), BF16)
        tables = [pltpu.VMEM((count, length, length), BF16)] * 2
        columns = pltpu.VMEM((width, count * PAIR), BF16)
        raw = pltpu.VMEM((count, length, SLOT), BF16)
        scores = pltpu.VMEM((count, length, CLUSTER), F32)
        back = tables + [columns, rows_s, pltpu.VMEM((count, length, PAIR), BF16), raw, pltpu.VMEM((2, length, width), BF16)]
        back += [scores, pltpu.VMEM((count, length, CLUSTER), BF16)]

        near_fields, near_probs, near_ctx, attn_sum, *near_orders = call(
            near_attention, [fields_t, probs_t, ctx_t, rows_f, *orders_t], [*tables, raw, scores, columns], 8,
            where_arg, layer_input, packed, c1, small, small_1, segment_ids, after=(small_2,),
        )
        small_3 = core_swap(small_2)
        c_far = relay(tie(c_first, attn_sum))
        c_far = (*c_far[:3], core_swap(c_far[3]))
        u_far = relay(tie(u_first, attn_sum))
        far_fields, far_probs, far_ctx, *far_orders, low, normed_a, inverse_a = call(
            far_attention, [fields_t, probs_t, ctx_t, *orders_t, rows_b, rows_f, ((length, 1), F32)],
            [*tables, raw, scores, columns, mat, mat, pltpu.VMEM((length, width), F32)], 1,
            where_arg, layer_input, *c_far, small_2, small_3, segment_ids, attn_sum, vecs,
        )
        u_far = (*u_far[:3], core_swap(tie(u_far[3], low)))
        d_far = relay(tie(d_first, low))
        near_hidden, near_slope, ffn_sum = call(
            near_forward, [pair_b, pair_b, rows_f], [], 6, low, up_weight, u1, down_weight, d1, small, small_1
        )
        far_hidden, far_slope = call(
            far_up, [pair_b, pair_b], [mat, mat], 5, where_arg, low, *u_far, small_2, small_3
        )
        d_far = (*d_far[:3], core_swap(tie(d_far[3], ffn_sum, far_hidden)))
        layer_output, grad_b, grad_b_low, sums_b = call(
            far_down, [rows_b, rows_f, rows_b, vec_t], [mat, mat], 5,
            where_arg, far_hidden, *d_far, ffn_sum, normed_a, out_cotangent, vecs,
        )
        dg3, dg2, dg1, dg0 = call(down_grads, [square] * 4, [], 2.8, far_hidden, near_hidden, grad_b_low)
        ds3, ds1 = core_swap(dg3), core_swap(dg1)
        ug3, ug2, grad_mid, far_ub = call(
            far_up_grads, [square, square, rows_f, vec_t], [mat] * 4 + [rows_s] * 2, 0.1,
            where_arg, grad_b_low, low, far_slope, *d_far, *u_far,
        )
        us3 = core_swap(ug3)
        down_cross = add(dg2, tie(ds3, grad_mid))
        ug1, ug0, grad_a, grad_a_low, near_ub, sums_a = call(
            near_up_grads, [square, square, rows_f, rows_b, vec_t, vec_t], [rows_s, rows_s, pltpu.VMEM((length, width), F32)], 0.1,
            grad_b_low, low, near_slope, down_weight, d1, up_weight, u1, grad_mid, grad_b, normed_a, inverse_a, vecs,
            after=(down_cross,),
        )
        us1 = core_swap(ug1)
        up_cross = add(ug2, tie(us3, grad_a_low))
        cg3, cg2, in_sum = call(
            far_attention_grads, [tall, tall, rows_f], back + [mat, mat], 0.1,
            where_arg, layer_input, grad_a_low, *c_far, *far_orders, far_fields, far_probs, far_ctx, sums_b, sums_a, far_ub,
            after=(up_cross,),
        )
        cs3 = core_swap(cg3)
        down_total = add(add(dg0, ds1), tie(chip_swap(down_cross), in_sum))
        packed_cross = add(cg2, cs3)
        cg1, cg0, input_grad = call(
            near_attention_grads, [tall, tall, rows_b], back, 0.1,
            layer_input, grad_a_low, packed, c1, *near_orders, near_fields, near_probs, near_ctx,
            sums_b, sums_a, near_ub, in_sum, grad_a, after=(down_total, packed_cross),
        )
        steps = [(level, True) for level in range(levels)] + [(level, False) for level in reversed(range(levels))]

        def step(total, at, *others):
            level, halve = steps[at]
            bit = (place >> level) & 1
            if halve:
                rows = total.shape[0] // 2
                send = lax.dynamic_slice_in_dim(total, (1 - bit) * rows, rows, axis=0)
                keep = lax.dynamic_slice_in_dim(total, bit * rows, rows, axis=0)
                return add(keep, tie(swap(send, "dp", level), *others))
            other = tie(swap(total, "dp", level), *others)
            return jnp.where(
                bit == 0, jnp.concatenate([total, other], axis=0), jnp.concatenate([other, total], axis=0)
            )

        last = len(steps) - 1
        down, up, whole = [down_total], [], []

        def reach(chain, at, *others):
            while len(chain) < min(at, last) + 2:
                chain.append(step(chain[-1], len(chain) - 1, *others))
            return chain[-1]

        reach(down, 0, input_grad)
        up.append(add(add(ug0, us1), tie(chip_swap(up_cross), down[-1])))
        reach(down, 2)
        reach(up, 0, down[-1])
        reach(down, 3, up[-1])
        whole.append(add(add(cg0, core_swap(cg1)), tie(chip_swap(packed_cross), down[-1], up[-1])))
        for at in range(last + 1):
            reach(down, max(4, at + 3))
            reach(up, at + 2 - (at > 1))
            reach(whole, at, down[-1], up[-1])
        down_grad, up_grad = [tie(chain[-1], whole[-2]).astype(F32) for chain in (down, up)]
        packed_grad = whole[-1]
        qkv_grad, out_grad, sums, qv_grad = call(
            unpack,
            [((3, heads * HEAD_DIM, width), F32), ((heads * HEAD_DIM, width), F32), ((16, width), F32),
             ((2, heads * HEAD_DIM), F32)],
            [pltpu.VMEM((3, heads * HEAD_DIM, width), F32), pltpu.SemaphoreType.DMA((3,))], 1, packed_grad, apart=1,
        )
        return (
            layer_output, input_grad, qkv_grad.transpose(0, 2, 1), qv_grad, out_grad, sums[5], sums[3], sums[4],
            up_grad, sums[6], down_grad, sums[2], sums[0], sums[1],
        )

    rows, split, copied = P(("dp", "tensor"), None), P(None, "tensor"), P()
    in_specs = (
        rows, rows, P(None, None, "tensor"), split, P("tensor", None), copied, copied, copied, split, P("tensor"),
        P("tensor", None), copied, copied, copied, P("dp", "tensor", None), P("dp", None),
    )
    out_specs = (
        rows, rows, P(None, None, "tensor"), split, P("tensor", None), copied, copied, copied, split, P("tensor"),
        P("tensor", None), copied, copied, copied,
    )
    return jax.shard_map(on_device, mesh=mesh, in_specs=in_specs, out_specs=out_specs, check_vma=False)
```
